32 devices in a mesh: samp: 8 (over z, y), var: 4 (over x, core).
Axes of the slice: x: 2, y: 2, z: 4, core: 2. Of those that a mesh axis runs over, the one named last changes fastest.
Arguments:
- geno: int32 [16384, 8192], P('samp', 'var'), may hold values from 0 to 2, as said below
- allele_pct: int32 [8192], P('var'), may hold values from 5 to 50
- test_geno: int32 [16384, 2048], P('samp', 'var'), may hold values from 0 to 2, as said below
- test_pct: int32 [2048], P('var'), may hold values from 5 to 50
- exposure: float32 [16384], P('samp'), may hold values from -4 to 4
- perm: int32 [8, 16384], P(None, 'samp'), may hold values from 0 to 16383, each once within a row
- var_comp: float32 [3], replicated, may hold values from 0.3 to 1.5
- solution: float32 [8, 16384], P(None, 'samp'), may hold values from -6 to 6
- resid: float32 [8, 16384], P(None, 'samp'), may hold values from -32 to 32
- direction: float32 [8, 16384], P(None, 'samp'), may hold values from -32 to 32
Outputs:
- new_solution: float32 [8, 16384], P(None, 'samp')
- new_resid: float32 [8, 16384], P(None, 'samp')
- new_direction: float32 [8, 16384], P(None, 'samp')
- assoc_scores: float32 [16, 2048], P(None, 'var')
The draws below stay inside these ranges and needn't reach their ends.
Inputs may be any that keep to these rules, and one draw needn't show every extreme that they name: `geno`: dosages of a variant follow its allele frequency. `test_geno`: dosages of a variant follow its allele frequency.
All inputs are finite; a program needn't handle non-finite values.
Results may differ from the reference program's by a relative error of at most 0.00016.
Values sent between devices are 32-bit elements; how exact they have to be, the bound alone decides.
No kernel may reach another device: no remote copies, remote signals or barrier semaphores. Data moves between devices by JAX's collectives and lax.ppermute only.
A program may use at most 64 MiB of HBM per device.

```python
import math
import jax
import jax.numpy as jnp
from jax import lax

SLAB = 8192
TESTV = 2048
RHS = 8
NS = 16384


def dosage_table(key, code, width):
    pct = jax.random.randint(jax.random.fold_in(key, code), (width,), 5, 51)
    draws = jax.random.randint(jax.random.fold_in(key, code + 1), (NS, width), 0, 10000)
    upper = 10000 - (100 - pct) * (100 - pct)
    double = pct * pct
    codes = (draws < upper[None, :]).astype(jnp.int32) + (draws < double[None, :]).astype(jnp.int32)
    return (pct.astype(jnp.int32), codes)


def draw_geno(key, part):
    return dosage_table(key, 101, SLAB)[1]


def draw_allele_pct(key, part):
    return dosage_table(key, 101, SLAB)[0]


def draw_test_geno(key, part):
    return dosage_table(key, 303, TESTV)[1]


def draw_test_pct(key, part):
    return dosage_table(key, 303, TESTV)[0]


def scaled_rows(key):
    position = jnp.arange(NS, dtype=jnp.float32) / max(NS - 1, 1)
    spread = jnp.exp(jax.random.uniform(jax.random.fold_in(key, 1), (NS,), jnp.float32, 0.0, 1.0) * math.log(10.0))
    column = jax.random.uniform(jax.random.fold_in(key, 2), (RHS, 1), jnp.float32, 0.5, 2.0)
    base = 0.1 * (1.0 + 2.0 * position) * spread
    values = jnp.clip(jax.random.normal(jax.random.fold_in(key, 4), (RHS, NS), jnp.float32), -4.0, 4.0)
    values = values * base[None, :] * column
    return values.astype(jnp.float32)


def draw_resid(key, part):
    return scaled_rows(jax.random.fold_in(key, 11))


def draw_direction(key, part):
    return scaled_rows(jax.random.fold_in(key, 23))


def level_of(own_key, extent, pieces, low, top_value):
    def one(dim, shards_of):
        heights = jax.random.uniform(jax.random.fold_in(jax.random.fold_in(own_key, 6), dim), (shards_of,), jnp.float32, low / len(pieces), top_value / len(pieces))
        return jnp.repeat(jnp.exp(heights), extent[dim] // shards_of).reshape((-1,) + (1,) * (len(extent) - dim - 1))

    factor_of = one(*pieces[0])
    for cut in pieces[1:]:
        factor_of = factor_of * one(*cut)
    return factor_of


def normal_values(stream_key, shape, scale, limit, cuts=(), kind=jnp.bfloat16):
    entries = jax.random.normal(stream_key, shape, jnp.float32) * scale
    if len(cuts) > 0:
        entries = level_of(stream_key, shape, cuts, -0.22, 0.18) * entries
    return jnp.clip(entries, min=-limit, max=limit).astype(kind)


def setup_inputs(seed: int = 0) -> dict:
    arg_keys = jax.random.split(jax.random.key(seed), 11)
    geno = draw_geno(jax.random.fold_in(arg_keys[10], 71), 0)
    allele_pct = draw_allele_pct(jax.random.fold_in(arg_keys[10], 71), 0)
    test_geno = draw_test_geno(jax.random.fold_in(arg_keys[10], 71), 0)
    test_pct = draw_test_pct(jax.random.fold_in(arg_keys[10], 71), 0)
    exposure = normal_values(arg_keys[4], (NS,), 1.0, 4.0, ((0, 8),), jnp.float32)
    perm = jax.vmap(lambda own: jax.random.permutation(own, NS))(jax.random.split(arg_keys[5], RHS)).reshape((RHS, NS)).astype(jnp.int32)
    var_comp = jnp.clip(jax.random.uniform(arg_keys[6], (3,), jnp.float32, 0.3, 1.5), 0.3, 1.5)
    solution = normal_values(arg_keys[7], (RHS, NS), 1.0, 6.0, ((1, 8),), jnp.float32)
    resid = draw_resid(jax.random.fold_in(arg_keys[10], 71), 0)
    direction = draw_direction(jax.random.fold_in(arg_keys[10], 71), 0)
    return dict(geno=geno, allele_pct=allele_pct, test_geno=test_geno, test_pct=test_pct, exposure=exposure, perm=perm, var_comp=var_comp, solution=solution, resid=resid, direction=direction)


def standardize(codes, pct):
    freq = pct.astype(jnp.float32) / 100.0
    return (codes.astype(jnp.float32) - 2.0 * freq) * lax.rsqrt(2.0 * freq * (1.0 - freq))

def reference(geno, allele_pct, test_geno, test_pct, exposure, perm, var_comp, solution, resid, direction):
    highest = lax.Precision.HIGHEST
    shuffled = exposure[perm]
    stacked = jnp.concatenate([direction, shuffled * direction], axis=0)
    block = math.gcd(SLAB, 1024)

    def add_block(index, total):
        start = index * block
        codes = lax.dynamic_slice_in_dim(geno, start, block, 1)
        pct = lax.dynamic_slice_in_dim(allele_pct, start, block, 0)
        loadings = standardize(codes, pct)
        weights = jnp.dot(stacked, loadings, precision=highest, preferred_element_type=jnp.float32)
        return total + lax.dot_general(weights, loadings, (((1,), (1,)), ((), ())), precision=highest, preferred_element_type=jnp.float32)
    kernel_rows = lax.fori_loop(0, SLAB // block, add_block, jnp.zeros((2 * RHS, NS), jnp.float32))
    image = var_comp[0] * direction + (var_comp[1] * kernel_rows[:RHS] + var_comp[2] * shuffled * kernel_rows[RHS:]) / SLAB
    norm_now = lax.optimization_barrier(jnp.sum(resid * resid, axis=1))
    curvature = lax.optimization_barrier(jnp.sum(direction * image, axis=1))
    alpha = norm_now / curvature
    new_solution = solution + alpha[:, None] * direction
    new_resid = resid - alpha[:, None] * image
    norm_next = lax.optimization_barrier(jnp.sum(new_resid * new_resid, axis=1))
    new_direction = new_resid + (norm_next / norm_now)[:, None] * direction
    markers = standardize(test_geno, test_pct)
    stacked_resid = jnp.concatenate([new_resid, shuffled * new_resid], axis=0)
    assoc_scores = jnp.dot(stacked_resid, markers, precision=highest, preferred_element_type=jnp.float32) / math.sqrt(NS)
    return (new_solution, new_resid, new_direction, assoc_scores)
```

```python
import functools
import math

import jax
import jax.numpy as jnp
from jax import lax
from jax.experimental import pallas as pl
from jax.experimental.pallas import tpu as pltpu
from jax.sharding import PartitionSpec as P

LANES = 128
ROWS = 8
VMEM_BYTES = 48 << 20
WHOLE = pl.BlockSpec(memory_space=pltpu.VMEM)
SCALARS = pl.BlockSpec(memory_space=pltpu.SMEM)


def in_vmem(shape, dtype=jnp.float32):
    return pltpu.VMEM(shape, dtype)


def call(body, out_shape, in_specs, **kwargs):
    return pl.pallas_call(
        body,
        out_shape=out_shape,
        in_specs=in_specs,
        compiler_params=pltpu.CompilerParams(vmem_limit_bytes=VMEM_BYTES),
        **kwargs,
    )


def bf16_pieces(x):
    pieces = []
    for _ in range(3):
        piece = x.astype(jnp.bfloat16)
        pieces.append(piece)
        x = x - piece.astype(jnp.float32)
    return jnp.concatenate(pieces, axis=0)


def add_pieces(y):
    rows = y.shape[0] // 3
    return y[:rows] + y[rows : 2 * rows] + y[2 * rows :]


def spread(pct):
    freq = pct.astype(jnp.float32) / 100.0
    return 2.0 * freq, lax.rsqrt(2.0 * freq * (1.0 - freq))


def cast_body(geno, test_geno, direction, codes, test_codes, total):
    step = pl.program_id(0)
    rows = geno.shape[0]
    here = pl.ds(pl.multiple_of(step * rows, rows), rows)
    block = geno[...].astype(jnp.float32).astype(jnp.bfloat16)
    codes[here, :] = block
    test_codes[here, :] = test_geno[...].astype(jnp.float32).astype(jnp.bfloat16)
    part = add_pieces(
        jnp.dot(bf16_pieces(direction[...]), block, preferred_element_type=jnp.float32)
    )

    @pl.when(step == 0)
    def _():
        total[...] = part

    @pl.when(step > 0)
    def _():
        total[...] += part


def cast_codes(geno, test_geno, direction):
    count, slab = geno.shape
    tests = test_geno.shape[1]
    rhs = direction.shape[0]
    rows = math.gcd(count, 512)
    return call(
        cast_body,
        [
            in_vmem((count, slab), jnp.bfloat16),
            in_vmem((count, tests), jnp.bfloat16),
            in_vmem((rhs, slab)),
        ],
        [
            pl.BlockSpec((rows, slab), lambda i: (i, 0)),
            pl.BlockSpec((rows, tests), lambda i: (i, 0)),
            pl.BlockSpec((rhs, rows), lambda i: (0, i)),
        ],
        grid=(count // rows,),
        out_specs=[WHOLE, WHOLE, WHOLE],
    )(geno, test_geno, direction)


def lookup(table, index, out):
    height = table.shape[0]
    rhs, count = index.shape
    left = add_columns(table[...])
    for b in range(rhs):
        places = index[b : b + 1, :]
        row = lax.broadcasted_iota(jnp.int32, (height, count), 0)
        chosen = jnp.where(row == places // LANES, 1.0, 0.0).astype(jnp.bfloat16)
        values = add_pieces(jnp.dot(left, chosen, preferred_element_type=jnp.float32))
        lane = lax.broadcasted_iota(jnp.int32, (LANES, count), 0)
        out[b : b + 1, :] = jnp.sum(
            jnp.where(lane == places % LANES, values, 0.0), axis=0, keepdims=True
        )


def add_columns(table):
    return bf16_pieces(table.T)


def slab_body(table, perm, direction, resid, codes, pct, raw, shuffled, sums):
    rhs, slab = raw.shape
    lookup(table, perm, shuffled)
    mean, scale = spread(pct[...])
    straight = direction[...]
    weighted = shuffled[...] * straight
    product = add_pieces(
        jnp.dot(bf16_pieces(weighted), codes[...], preferred_element_type=jnp.float32)
    )
    sums[:rhs, :slab] = scale * (raw[...] - mean * jnp.sum(straight, axis=1, keepdims=True))
    sums[rhs:, :slab] = scale * (product - mean * jnp.sum(weighted, axis=1, keepdims=True))
    left = resid[...]
    norm = jnp.sum(left * left, axis=1, keepdims=True)
    length = jnp.sum(straight * straight, axis=1, keepdims=True)
    sums[:rhs, slab:] = jnp.broadcast_to(norm, (rhs, LANES))
    sums[rhs:, slab:] = jnp.broadcast_to(length, (rhs, LANES))


def slab_sums(table, perm, direction, resid, codes, pct, raw):
    rhs, slab = raw.shape
    return call(
        slab_body,
        [in_vmem(perm.shape), in_vmem((2 * rhs, slab + LANES))],
        [WHOLE] * 7,
        out_specs=[WHOLE, WHOLE],
    )(table, perm, direction, resid, codes, pct, raw)


def kernel_body(parts, codes, pct, shuffled, var_comp, slab_total, out):
    rhs, count = shuffled.shape
    slab = pct.shape[1]
    sums = parts[:, :slab]
    mean, scale = spread(pct[...])
    weights = scale * sums
    product = add_pieces(
        lax.dot_general(
            bf16_pieces(weights),
            codes[...],
            (((1,), (1,)), ((), ())),
            preferred_element_type=jnp.float32,
        )
    ) - jnp.sum(mean * weights, axis=1, keepdims=True)
    share = 1.0 / slab_total
    out[:, :count] = (
        var_comp[1] * product[:rhs] + var_comp[2] * shuffled[...] * product[rhs:]
    ) * share
    squares = jnp.sum(sums * sums, axis=1, keepdims=True)
    energy = (var_comp[1] * squares[:rhs] + var_comp[2] * squares[rhs:]) * share
    out[:, count:] = jnp.broadcast_to(energy, (rhs, LANES))


def kernel_part(parts, codes, pct, shuffled, var_comp, slab_total):
    rhs, count = shuffled.shape

    def body(parts, codes, pct, shuffled, var_comp, out):
        kernel_body(parts, codes, pct, shuffled, var_comp, slab_total, out)

    return call(
        body,
        in_vmem((rhs, count + LANES)),
        [WHOLE, WHOLE, WHOLE, WHOLE, SCALARS],
        out_specs=WHOLE,
    )(parts, codes, pct, shuffled, var_comp)


def step_body(applied, parts, shuffled, direction, resid, solution, codes, pct, var_comp,
              new_solution, new_resid, scores, root):
    rhs, count = shuffled.shape
    tests = pct.shape[1]
    norms = parts[...]
    straight = direction[...]
    image = var_comp[0] * straight + applied[:, :count]
    curvature = var_comp[0] * norms[rhs:, :1] + applied[:, count : count + 1]
    alpha = norms[:rhs, :1] / curvature
    left = resid[...] - alpha * image
    new_resid[...] = left
    new_solution[...] = solution[...] + alpha * straight
    both = jnp.concatenate([left, shuffled[...] * left], axis=0)
    mean, scale = spread(pct[...])
    product = add_pieces(
        jnp.dot(bf16_pieces(both), codes[...], preferred_element_type=jnp.float32)
    )
    scores[:, :tests] = (scale / root) * (product - mean * jnp.sum(both, axis=1, keepdims=True))
    norm = jnp.sum(left * left, axis=1, keepdims=True)
    scores[:rhs, tests:] = jnp.broadcast_to(norm, (rhs, LANES))
    scores[rhs:, tests:] = jnp.zeros((rhs, LANES), jnp.float32)


def step(applied, norms, shuffled, direction, resid, solution, codes, pct, var_comp, root):
    rhs, count = shuffled.shape
    tests = pct.shape[1]
    return call(
        functools.partial(step_body, root=root),
        [in_vmem((rhs, count)), in_vmem((rhs, count)), in_vmem((2 * rhs, tests + LANES))],
        [WHOLE] * 8 + [SCALARS],
        out_specs=[WHOLE] * 3,
    )(applied, norms, shuffled, direction, resid, solution, codes, pct, var_comp)


def gather_all(x, axis):
    size = lax.axis_size(axis)
    copies = jnp.broadcast_to(x[None], (size, *x.shape))
    return lax.all_to_all(copies, axis, 0, 0)


def swap(x, axis, distance):
    size = lax.axis_size(axis)
    return lax.ppermute(x, axis, [(i, i ^ distance) for i in range(size)])


def sum_all(x, axis, widths):
    size = lax.axis_size(axis)
    if size & (size - 1):
        return lax.psum(x, axis)
    unit = 1
    for width in widths(size):
        if width == 2:
            x = x + swap(x, axis, unit)
        else:
            near, far, last = (swap(x, axis, k * unit) for k in (1, 2, 3))
            x = (x + near) + (far + last)
        unit *= width
    return x


def pairs_then_fours(size):
    bits = size.bit_length() - 1
    return [2] * (bits % 2) + [4] * (bits // 2)


def pairs(size):
    return [2] * (size.bit_length() - 1)


def local(
    geno, allele_pct, test_geno, test_pct, exposure, perm, var_comp, solution, resid, direction
):
    rhs, count = resid.shape
    slab = geno.shape[1]
    tests = test_geno.shape[1]
    table = gather_all(exposure.reshape(-1, LANES), "samp").reshape(-1, LANES)
    codes, test_codes, raw = cast_codes(geno, test_geno, direction)
    pct = allele_pct.reshape(1, slab)
    shuffled, sums = slab_sums(table, perm, direction, resid, codes, pct, raw)
    sums = sum_all(sums, "samp", pairs_then_fours)
    applied = kernel_part(
        sums, codes, pct, shuffled, var_comp, float(slab * lax.axis_size("var"))
    )
    applied = sum_all(applied, "var", pairs)
    norms = sums[:, slab:]
    new_solution, new_resid, scores = step(
        applied, norms, shuffled, direction, resid, solution, test_codes,
        test_pct.reshape(1, tests), var_comp, math.sqrt(count * lax.axis_size("samp")),
    )
    scores = sum_all(scores, "samp", pairs_then_fours)
    ratio = scores[:rhs, tests : tests + 1] / norms[:rhs, :1]
    new_direction = new_resid + ratio * direction
    return (new_solution, new_resid, new_direction, scores[:, :tests])


def solution(mesh):
    return jax.shard_map(
        local,
        mesh=mesh,
        in_specs=(
            P("samp", "var"),
            P("var"),
            P("samp", "var"),
            P("var"),
            P("samp"),
            P(None, "samp"),
            P(),
            P(None, "samp"),
            P(None, "samp"),
            P(None, "samp"),
        ),
        out_specs=(P(None, "samp"), P(None, "samp"), P(None, "samp"), P(None, "var")),
        check_vma=False,
    )
```

```python
import functools
import math

import jax
import jax.numpy as jnp
from jax import lax
from jax.experimental import pallas as pl
from jax.experimental.pallas import tpu as pltpu
from jax.sharding import PartitionSpec as P

LANES = 128
CAST_ROWS = 64
VMEM_BYTES = 10 << 20
WHOLE = pl.BlockSpec(memory_space=pltpu.VMEM)
SCALARS = pl.BlockSpec(memory_space=pltpu.SMEM)


def in_vmem(shape, dtype=jnp.float32):
    return pltpu.VMEM(shape, dtype)


def call(body, out_shape, in_specs, **kwargs):
    return pl.pallas_call(
        body,
        out_shape=out_shape,
        in_specs=in_specs,
        out_specs=jax.tree.map(lambda _: WHOLE, out_shape),
        compiler_params=pltpu.CompilerParams(vmem_limit_bytes=VMEM_BYTES),
        **kwargs,
    )


def bf16_pieces(x):
    pieces = []
    for _ in range(3):
        piece = x.astype(jnp.bfloat16)
        pieces.append(piece)
        x = x - piece.astype(jnp.float32)
    return jnp.concatenate(pieces, axis=0)


def add_pieces(y):
    rows = y.shape[0] // 3
    return y[:rows] + y[rows : 2 * rows] + y[2 * rows :]


def spread(pct):
    freq = pct.astype(jnp.float32) / 100.0
    return 2.0 * freq, lax.rsqrt(2.0 * freq * (1.0 - freq))


def cast_body(geno, codes):
    rows = math.gcd(geno.shape[0], CAST_ROWS)

    @pl.loop(0, geno.shape[0] // rows)
    def _(step):
        here = pl.ds(pl.multiple_of(step * rows, rows), rows)
        codes[here, :] = geno[here, :].astype(jnp.float32).astype(jnp.bfloat16)


def cast_codes(geno):
    return call(cast_body, in_vmem(geno.shape, jnp.bfloat16), [WHOLE])(geno)


def stack_body(*refs):
    *blocks, out = refs
    out[...] = jnp.concatenate([block[...] for block in blocks], axis=0)


def stack(blocks):
    rows = sum(block.shape[0] for block in blocks)
    return call(
        stack_body,
        in_vmem((rows, LANES)),
        [WHOLE] * len(blocks),
        cost_estimate=pl.CostEstimate(flops=1 << 34, bytes_accessed=1 << 25, transcendentals=0),
    )(*blocks)


def lookup(table, index, out):
    height = table.shape[0]
    rhs, count = index.shape
    exact = jnp.bfloat16 if height <= 256 else jnp.float32
    row = lax.broadcasted_iota(jnp.int32, (height, count), 0).astype(exact)
    lane = lax.broadcasted_iota(jnp.int32, (LANES, count), 0)
    high, middle, low = jnp.split(bf16_pieces(table.T), 3, axis=0)
    left = jnp.concatenate(
        [
            jnp.concatenate([high, middle], axis=1),
            jnp.concatenate([low, jnp.zeros_like(low)], axis=1),
        ],
        axis=0,
    )
    for b in range(rhs):
        places = index[b : b + 1, :]
        wanted = (places // LANES).astype(jnp.float32).astype(exact)
        one, none = jnp.ones((), exact), jnp.zeros((), exact)
        chosen = jnp.where(row == wanted, one, none).astype(jnp.bfloat16)
        values = jnp.dot(
            left,
            jnp.concatenate([chosen, chosen], axis=0),
            preferred_element_type=jnp.float32,
        )
        values = values[:LANES] + values[LANES:]
        out[b : b + 1, :] = jnp.sum(
            jnp.where(lane == places % LANES, values, 0.0), axis=0, keepdims=True
        )


def slab_body(perm, direction, resid, codes, pct, *refs, axis):
    *table, shuffled, sums = refs
    rhs = direction.shape[0]
    slab = codes.shape[1]
    table = jnp.concatenate([block[...] for block in table], axis=0)
    shard = table.size // lax.axis_size(axis)
    lookup(table, perm[...] ^ (lax.axis_index(axis) * shard), shuffled)
    mean, scale = spread(pct[...])
    straight = direction[...]
    both = jnp.concatenate([straight, shuffled[...] * straight], axis=0)
    product = add_pieces(
        jnp.dot(bf16_pieces(both), codes[...], preferred_element_type=jnp.float32)
    )
    sums[:, :slab] = scale * (product - mean * jnp.sum(both, axis=1, keepdims=True))
    left = resid[...]
    norm = jnp.sum(left * left, axis=1, keepdims=True)
    length = jnp.sum(straight * straight, axis=1, keepdims=True)
    sums[:rhs, slab:] = jnp.broadcast_to(norm, (rhs, LANES))
    sums[rhs:, slab:] = jnp.broadcast_to(length, (rhs, LANES))


def slab_sums(table, perm, direction, resid, codes, pct, axis):
    rhs, slab = direction.shape[0], codes.shape[1]
    return call(
        functools.partial(slab_body, axis=axis),
        [in_vmem(perm.shape), in_vmem((2 * rhs, slab + LANES))],
        [WHOLE] * (5 + len(table)),
    )(perm, direction, resid, codes, pct, *table)


def kernel_body(sums, codes, pct, shuffled, var_comp, out, *, slab_total):
    rhs, count = shuffled.shape
    slab = codes.shape[1]
    weights = sums[:, :slab]
    squares = jnp.sum(weights * weights, axis=1, keepdims=True)
    mean, scale = spread(pct[...])
    weights = scale * weights
    product = add_pieces(
        lax.dot_general(
            bf16_pieces(weights),
            codes[...],
            (((1,), (1,)), ((), ())),
            preferred_element_type=jnp.float32,
        )
    ) - jnp.sum(mean * weights, axis=1, keepdims=True)
    share = 1.0 / slab_total
    out[:, :count] = (
        var_comp[1] * product[:rhs] + var_comp[2] * shuffled[...] * product[rhs:]
    ) * share
    energy = (var_comp[1] * squares[:rhs] + var_comp[2] * squares[rhs:]) * share
    out[:, count:] = jnp.broadcast_to(energy, (rhs, LANES))


def kernel_part(sums, codes, pct, shuffled, var_comp, slab_total):
    rhs, count = shuffled.shape
    return call(
        functools.partial(kernel_body, slab_total=slab_total),
        in_vmem((rhs, count + LANES)),
        [WHOLE] * 4 + [SCALARS],
    )(sums, codes, pct, shuffled, var_comp)


def step_body(applied, sums, shuffled, direction, resid, solution, codes, pct, var_comp,
              new_solution, new_resid, scores, *, root):
    rhs, count = shuffled.shape
    tests = codes.shape[1]
    norms = sums[:, -LANES:]
    straight = direction[...]
    image = var_comp[0] * straight + applied[:, :count]
    curvature = var_comp[0] * norms[rhs:, :1] + applied[:, count : count + 1]
    alpha = norms[:rhs, :1] / curvature
    left = resid[...] - alpha * image
    new_resid[...] = left
    new_solution[...] = solution[...] + alpha * straight
    both = jnp.concatenate([left, shuffled[...] * left], axis=0)
    mean, scale = spread(pct[...])
    product = add_pieces(
        jnp.dot(bf16_pieces(both), codes[...], preferred_element_type=jnp.float32)
    )
    scores[:, :tests] = (scale / root) * (product - mean * jnp.sum(both, axis=1, keepdims=True))
    norm = jnp.sum(left * left, axis=1, keepdims=True)
    scores[:rhs, tests:] = jnp.broadcast_to(norm, (rhs, LANES))
    scores[rhs:, tests:] = jnp.zeros((rhs, LANES), jnp.float32)


def step(applied, sums, shuffled, direction, resid, solution, codes, pct, var_comp, root):
    rhs, count = shuffled.shape
    return call(
        functools.partial(step_body, root=root),
        [
            in_vmem((rhs, count)),
            in_vmem((rhs, count)),
            in_vmem((2 * rhs, codes.shape[1] + LANES)),
        ],
        [WHOLE] * 8 + [SCALARS],
    )(applied, sums, shuffled, direction, resid, solution, codes, pct, var_comp)


def finish_body(sums, new_resid, direction, *refs):
    *parts, new_direction, scores = refs
    rhs = direction.shape[0]
    tests = scores.shape[1]
    total = add_parts([part[...] for part in parts])
    scores[...] = total[:, :tests]
    ratio = total[:rhs, tests : tests + 1] / sums[:rhs, -LANES:][:, :1]
    new_direction[...] = new_resid[...] + ratio * direction[...]


def finish(parts, sums, new_resid, direction):
    rows, columns = parts[0].shape
    return call(
        finish_body,
        [
            jax.ShapeDtypeStruct(direction.shape, jnp.float32),
            jax.ShapeDtypeStruct((rows, columns - LANES), jnp.float32),
        ],
        [WHOLE] * (3 + len(parts)),
    )(sums, new_resid, direction, *parts)


def swap(x, axis, distance):
    size = lax.axis_size(axis)
    return lax.ppermute(x, axis, [(i, i ^ distance) for i in range(size)])


def add_parts(parts):
    if len(parts) == 4:
        return (parts[0] + parts[1]) + (parts[2] + parts[3])
    return sum(parts[1:], parts[0])


def sum_parts(x, axis, widths):
    parts = [x]
    unit = 1
    for width in widths(lax.axis_size(axis)):
        held = add_parts(parts)
        parts = [held] + [swap(held, axis, k * unit) for k in range(1, width)]
        unit *= width
    return parts


def sum_all(x, axis, widths):
    return add_parts(sum_parts(x, axis, widths))


def gather_all(x, axis, widths):
    blocks = [x]
    unit = 1
    for width in widths(lax.axis_size(axis)):
        held = blocks[0] if len(blocks) == 1 else stack(blocks)
        blocks = [held] + [swap(held, axis, k * unit) for k in range(1, width)]
        unit *= width
    return blocks


def pairs_then_fours(size):
    bits = size.bit_length() - 1
    return [2] * (bits % 2) + [4] * (bits // 2)


def pairs(size):
    return [2] * (size.bit_length() - 1)


def local(
    geno, allele_pct, test_geno, test_pct, exposure, perm, var_comp, solution, resid, direction
):
    count = resid.shape[1]
    slab = geno.shape[1]
    tests = test_geno.shape[1]
    slab_total = float(slab * lax.axis_size("var"))
    root = math.sqrt(count * lax.axis_size("samp"))
    pct = allele_pct.reshape(1, slab)
    table = gather_all(exposure.reshape(-1, LANES), "samp", pairs_then_fours)
    codes = cast_codes(geno)
    shuffled, sums = slab_sums(table, perm, direction, resid, codes, pct, "samp")
    sums = sum_all(sums, "samp", pairs_then_fours)
    applied = kernel_part(sums, codes, pct, shuffled, var_comp, slab_total)
    applied = sum_all(applied, "var", pairs)
    test_codes = cast_codes(test_geno)
    new_solution, new_resid, scores = step(
        applied, sums, shuffled, direction, resid, solution, test_codes,
        test_pct.reshape(1, tests), var_comp, root,
    )
    parts = sum_parts(scores, "samp", pairs_then_fours)
    new_direction, scores = finish(parts, sums, new_resid, direction)
    return (new_solution, new_resid, new_direction, scores)


def solution(mesh):
    return jax.shard_map(
        local,
        mesh=mesh,
        in_specs=(
            P("samp", "var"),
            P("var"),
            P("samp", "var"),
            P("var"),
            P("samp"),
            P(None, "samp"),
            P(),
            P(None, "samp"),
            P(None, "samp"),
            P(None, "samp"),
        ),
        out_specs=(P(None, "samp"), P(None, "samp"), P(None, "samp"), P(None, "var")),
        check_vma=False,
    )
```

```python
import functools
import math

import jax
import jax.numpy as jnp
from jax import lax
from jax.experimental import pallas as pl
from jax.experimental.pallas import tpu as pltpu
from jax.sharding import PartitionSpec as P

LANES = 128
CAST_ROWS = 64
FLIP_ROWS = 512
VMEM_BYTES = 10 << 20
WHOLE = pl.BlockSpec(memory_space=pltpu.VMEM)
SCALARS = pl.BlockSpec(memory_space=pltpu.SMEM)


def in_vmem(shape, dtype=jnp.float32):
    return pltpu.VMEM(shape, dtype)


def call(body, out_shape, in_specs, **kwargs):
    return pl.pallas_call(
        body,
        out_shape=out_shape,
        in_specs=in_specs,
        out_specs=jax.tree.map(lambda _: WHOLE, out_shape),
        compiler_params=pltpu.CompilerParams(vmem_limit_bytes=VMEM_BYTES),
        **kwargs,
    )


def cost(products):
    return pl.CostEstimate(flops=8 * products, bytes_accessed=0, transcendentals=0)


def bf16_pieces(x):
    pieces = []
    for _ in range(3):
        piece = x.astype(jnp.bfloat16)
        pieces.append(piece)
        x = x - piece.astype(jnp.float32)
    return jnp.concatenate(pieces, axis=0)


def add_pieces(y):
    rows = y.shape[0] // 3
    return y[:rows] + y[rows : 2 * rows] + y[2 * rows :]


def spread(pct):
    freq = pct.astype(jnp.float32) / 100.0
    return 2.0 * freq, lax.rsqrt(2.0 * freq * (1.0 - freq))


def cast_body(geno, codes):
    rows = math.gcd(geno.shape[0], CAST_ROWS)

    @pl.loop(0, geno.shape[0] // rows)
    def _(step):
        here = pl.ds(pl.multiple_of(step * rows, rows), rows)
        codes[here, :] = geno[here, :].astype(jnp.float32).astype(jnp.bfloat16)


def cast_codes(geno):
    return call(cast_body, in_vmem(geno.shape, jnp.bfloat16), [WHOLE])(geno)


def flip_body(codes, flipped, *, start):
    rows = math.gcd(codes.shape[0], FLIP_ROWS)
    columns = slice(start, start + flipped.shape[0])

    @pl.loop(0, codes.shape[0] // rows)
    def _(step):
        here = pl.ds(pl.multiple_of(step * rows, rows), rows)
        flipped[:, here] = codes[here, columns].T


def flip_codes(codes, start, width):
    return call(
        functools.partial(flip_body, start=start),
        in_vmem((width, codes.shape[0]), codes.dtype),
        [WHOLE],
        cost_estimate=cost(64 * codes.shape[0] * width),
    )(codes)


def stack_body(*refs):
    *blocks, out = refs
    out[...] = jnp.concatenate([block[...] for block in blocks], axis=0)


def stack(blocks):
    rows = sum(block.shape[0] for block in blocks)
    return call(
        stack_body,
        in_vmem((rows, LANES)),
        [WHOLE] * len(blocks),
        cost_estimate=pl.CostEstimate(flops=1 << 34, bytes_accessed=1 << 25, transcendentals=0),
    )(*blocks)


def lookup(table, index, out):
    height = table.shape[0]
    rhs, count = index.shape
    exact = jnp.bfloat16 if height <= 256 else jnp.float32
    row = lax.broadcasted_iota(jnp.int32, (height, count), 0).astype(exact)
    lane = lax.broadcasted_iota(jnp.int32, (LANES, count), 0)
    high, middle, low = jnp.split(bf16_pieces(table.T), 3, axis=0)
    left = jnp.concatenate(
        [
            jnp.concatenate([high, middle], axis=1),
            jnp.concatenate([low, jnp.zeros_like(low)], axis=1),
        ],
        axis=0,
    )
    for b in range(rhs):
        places = index[b : b + 1, :]
        wanted = (places // LANES).astype(jnp.float32).astype(exact)
        one, none = jnp.ones((), exact), jnp.zeros((), exact)
        chosen = jnp.where(row == wanted, one, none).astype(jnp.bfloat16)
        values = jnp.dot(
            left,
            jnp.concatenate([chosen, chosen], axis=0),
            preferred_element_type=jnp.float32,
        )
        values = values[:LANES] + values[LANES:]
        out[b : b + 1, :] = jnp.sum(
            jnp.where(lane == places % LANES, values, 0.0), axis=0, keepdims=True
        )


def slab_body(perm, direction, resid, codes, pct, *refs, axis):
    *table, shuffled, sums = refs
    rhs = direction.shape[0]
    slab = codes.shape[1]
    table = jnp.concatenate([block[...] for block in table], axis=0)
    shard = table.size // lax.axis_size(axis)
    lookup(table, perm[...] ^ (lax.axis_index(axis) * shard), shuffled)
    mean, scale = spread(pct[...])
    straight = direction[...]
    both = jnp.concatenate([straight, shuffled[...] * straight], axis=0)
    product = add_pieces(
        jnp.dot(bf16_pieces(both), codes[...], preferred_element_type=jnp.float32)
    )
    sums[:, :slab] = scale * (product - mean * jnp.sum(both, axis=1, keepdims=True))
    left = resid[...]
    norm = jnp.sum(left * left, axis=1, keepdims=True)
    length = jnp.sum(straight * straight, axis=1, keepdims=True)
    sums[:rhs, slab:] = jnp.broadcast_to(norm, (rhs, LANES))
    sums[rhs:, slab:] = jnp.broadcast_to(length, (rhs, LANES))


def slab_sums(table, perm, direction, resid, codes, pct, axis):
    rhs, slab = direction.shape[0], codes.shape[1]
    return call(
        functools.partial(slab_body, axis=axis),
        [in_vmem(perm.shape), in_vmem((2 * rhs, slab + LANES))],
        [WHOLE] * (5 + len(table)),
    )(perm, direction, resid, codes, pct, *table)


def kernel_body(sums, flipped, pct, shuffled, var_comp, out, *, slab_total):
    rhs, count = shuffled.shape
    slab = flipped.shape[0]
    weights = sums[:, :slab]
    squares = jnp.sum(weights * weights, axis=1, keepdims=True)
    mean, scale = spread(pct[...])
    weights = scale * weights
    product = add_pieces(
        jnp.dot(bf16_pieces(weights), flipped[...], preferred_element_type=jnp.float32)
    ) - jnp.sum(mean * weights, axis=1, keepdims=True)
    share = 1.0 / slab_total
    out[:, :count] = (
        var_comp[1] * product[:rhs] + var_comp[2] * shuffled[...] * product[rhs:]
    ) * share
    energy = (var_comp[1] * squares[:rhs] + var_comp[2] * squares[rhs:]) * share
    out[:, count:] = jnp.broadcast_to(energy, (rhs, LANES))


def kernel_part(sums, flipped, pct, shuffled, var_comp, slab_total):
    rhs, count = shuffled.shape
    return call(
        functools.partial(kernel_body, slab_total=slab_total),
        in_vmem((rhs, count + LANES)),
        [WHOLE] * 4 + [SCALARS],
    )(sums, flipped, pct, shuffled, var_comp)


def step_body(applied, sums, shuffled, direction, resid, solution, codes, pct, var_comp,
              new_solution, new_resid, scores, *, root):
    rhs, count = shuffled.shape
    tests = codes.shape[1]
    norms = sums[:, -LANES:]
    straight = direction[...]
    image = var_comp[0] * straight + applied[:, :count]
    curvature = var_comp[0] * norms[rhs:, :1] + applied[:, count : count + 1]
    alpha = norms[:rhs, :1] / curvature
    left = resid[...] - alpha * image
    new_resid[...] = left
    new_solution[...] = solution[...] + alpha * straight
    both = jnp.concatenate([left, shuffled[...] * left], axis=0)
    mean, scale = spread(pct[...])
    product = add_pieces(
        jnp.dot(bf16_pieces(both), codes[...], preferred_element_type=jnp.float32)
    )
    scores[:, :tests] = (scale / root) * (product - mean * jnp.sum(both, axis=1, keepdims=True))
    norm = jnp.sum(left * left, axis=1, keepdims=True)
    scores[:rhs, tests:] = jnp.broadcast_to(norm, (rhs, LANES))
    scores[rhs:, tests:] = jnp.zeros((rhs, LANES), jnp.float32)


def step(applied, sums, shuffled, direction, resid, solution, codes, pct, var_comp, root):
    rhs, count = shuffled.shape
    return call(
        functools.partial(step_body, root=root),
        [
            in_vmem((rhs, count)),
            in_vmem((rhs, count)),
            in_vmem((2 * rhs, codes.shape[1] + LANES)),
        ],
        [WHOLE] * 8 + [SCALARS],
    )(applied, sums, shuffled, direction, resid, solution, codes, pct, var_comp)


def finish_body(sums, new_resid, direction, *refs):
    *parts, new_direction, scores = refs
    rhs = direction.shape[0]
    tests = scores.shape[1]
    total = add_parts([part[...] for part in parts])
    scores[...] = total[:, :tests]
    ratio = total[:rhs, tests : tests + 1] / sums[:rhs, -LANES:][:, :1]
    new_direction[...] = new_resid[...] + ratio * direction[...]


def finish(parts, sums, new_resid, direction):
    rows, columns = parts[0].shape
    return call(
        finish_body,
        [
            jax.ShapeDtypeStruct(direction.shape, jnp.float32),
            jax.ShapeDtypeStruct((rows, columns - LANES), jnp.float32),
        ],
        [WHOLE] * (3 + len(parts)),
    )(sums, new_resid, direction, *parts)


def swap(x, axis, distance):
    size = lax.axis_size(axis)
    return lax.ppermute(x, axis, [(i, i ^ distance) for i in range(size)])


def add_parts(parts):
    if len(parts) == 4:
        return (parts[0] + parts[1]) + (parts[2] + parts[3])
    return sum(parts[1:], parts[0])


def sum_parts(x, axis, widths, unit=1):
    parts = [x]
    for width in widths(lax.axis_size(axis) // unit):
        held = add_parts(parts)
        parts = [held] + [swap(held, axis, k * unit) for k in range(1, width)]
        unit *= width
    return parts


def sum_all(x, axis, widths, unit=1):
    return add_parts(sum_parts(x, axis, widths, unit))


def gather_all(x, axis, widths):
    blocks = [x]
    unit = 1
    for width in widths(lax.axis_size(axis)):
        held = blocks[0] if len(blocks) == 1 else stack(blocks)
        blocks = [held] + [swap(held, axis, k * unit) for k in range(1, width)]
        unit *= width
    return blocks


def pairs_then_fours(size):
    bits = size.bit_length() - 1
    return [2] * (bits % 2) + [4] * (bits // 2)


def pairs(size):
    return [2] * (size.bit_length() - 1)


def local(
    geno, allele_pct, test_geno, test_pct, exposure, perm, var_comp, solution, resid, direction
):
    count = resid.shape[1]
    slab = geno.shape[1]
    tests = test_geno.shape[1]
    slab_total = float(slab * lax.axis_size("var"))
    root = math.sqrt(count * lax.axis_size("samp"))
    pct = allele_pct.reshape(1, slab)
    table = gather_all(exposure.reshape(-1, LANES), "samp", pairs_then_fours)
    codes = cast_codes(geno)
    shuffled, sums = slab_sums(table, perm, direction, resid, codes, pct, "samp")
    sums = sums + swap(sums, "samp", 1)
    codes, sums = lax.optimization_barrier((codes, sums))
    flipped = flip_codes(codes, 0, slab)
    sums = sum_all(sums, "samp", pairs_then_fours, 2)
    applied = kernel_part(sums, flipped, pct, shuffled, var_comp, slab_total)
    applied = sum_all(applied, "var", pairs)
    test_codes = cast_codes(test_geno)
    new_solution, new_resid, scores = step(
        applied, sums, shuffled, direction, resid, solution, test_codes,
        test_pct.reshape(1, tests), var_comp, root,
    )
    parts = sum_parts(scores, "samp", pairs_then_fours)
    new_direction, scores = finish(parts, sums, new_resid, direction)
    return (new_solution, new_resid, new_direction, scores)


def solution(mesh):
    return jax.shard_map(
        local,
        mesh=mesh,
        in_specs=(
            P("samp", "var"),
            P("var"),
            P("samp", "var"),
            P("var"),
            P("samp"),
            P(None, "samp"),
            P(),
            P(None, "samp"),
            P(None, "samp"),
            P(None, "samp"),
        ),
        out_specs=(P(None, "samp"), P(None, "samp"), P(None, "samp"), P(None, "var")),
        check_vma=False,
    )
```

```python
import functools
import math

import jax
import jax.numpy as jnp
from jax import lax
from jax.experimental import pallas as pl
from jax.experimental.pallas import tpu as pltpu
from jax.sharding import PartitionSpec as P

LANES = 128
CAST_ROWS = 64
FLIP_ROWS = 512
VMEM_BYTES = 10 << 20
WHOLE = pl.BlockSpec(memory_space=pltpu.VMEM)
SCALARS = pl.BlockSpec(memory_space=pltpu.SMEM)


def in_vmem(shape, dtype=jnp.float32):
    return pltpu.VMEM(shape, dtype)


def call(body, out_shape, in_specs, **kwargs):
    return pl.pallas_call(
        body,
        out_shape=out_shape,
        in_specs=in_specs,
        out_specs=jax.tree.map(lambda _: WHOLE, out_shape),
        compiler_params=pltpu.CompilerParams(vmem_limit_bytes=VMEM_BYTES),
        **kwargs,
    )


def cost(products):
    return pl.CostEstimate(flops=8 * products, bytes_accessed=0, transcendentals=0)


def bf16_pieces(x):
    pieces = []
    for _ in range(3):
        piece = x.astype(jnp.bfloat16)
        pieces.append(piece)
        x = x - piece.astype(jnp.float32)
    return jnp.concatenate(pieces, axis=0)


def add_pieces(y):
    rows = y.shape[0] // 3
    return y[:rows] + y[rows : 2 * rows] + y[2 * rows :]


def spread(pct):
    freq = pct.astype(jnp.float32) / 100.0
    return 2.0 * freq, lax.rsqrt(2.0 * freq * (1.0 - freq))


def cast_body(geno, codes):
    rows = math.gcd(geno.shape[0], CAST_ROWS)

    @pl.loop(0, geno.shape[0] // rows)
    def _(step):
        here = pl.ds(pl.multiple_of(step * rows, rows), rows)
        codes[here, :] = geno[here, :].astype(jnp.float32).astype(jnp.bfloat16)


def cast_codes(geno):
    return call(cast_body, in_vmem(geno.shape, jnp.bfloat16), [WHOLE])(geno)


def flip_body(codes, flipped, *, start):
    rows = math.gcd(codes.shape[0], FLIP_ROWS)
    columns = slice(start, start + flipped.shape[0])

    @pl.loop(0, codes.shape[0] // rows)
    def _(step):
        here = pl.ds(pl.multiple_of(step * rows, rows), rows)
        flipped[:, here] = codes[here, columns].T


def flip_codes(codes, start, width):
    return call(
        functools.partial(flip_body, start=start),
        in_vmem((width, codes.shape[0]), codes.dtype),
        [WHOLE],
        cost_estimate=cost(64 * codes.shape[0] * width),
    )(codes)


def blank_body(out):
    out[...] = jnp.zeros_like(out)


def blank(rows):
    early = pl.CostEstimate(flops=1 << 34, bytes_accessed=1 << 25, transcendentals=0)
    return call(blank_body, in_vmem((rows, LANES)), [], cost_estimate=early)()


def stack_body(*refs):
    *blocks, out = refs
    out[...] = jnp.concatenate([block[...] for block in blocks], axis=0)


def stack(blocks):
    rows = sum(block.shape[0] for block in blocks)
    return call(stack_body, in_vmem((rows, LANES)), [WHOLE] * len(blocks))(*blocks)


def lookup(table, index, out):
    height = table.shape[0]
    rhs, count = index.shape
    half = LANES // 2
    exact = jnp.bfloat16 if 2 * height <= 256 else jnp.float32
    row = lax.broadcasted_iota(jnp.int32, (2 * height, count), 0).astype(exact)
    lane = lax.broadcasted_iota(jnp.int32, (half, count), 0)
    halves = table.T
    left = bf16_pieces(jnp.concatenate([halves[:half], halves[half:]], axis=1))
    one, none = jnp.ones((), exact), jnp.zeros((), exact)
    for b in range(rhs):
        places = index[b : b + 1, :]
        wanted = places // LANES + height * (places // half % 2)
        chosen = jnp.where(row == wanted.astype(jnp.float32).astype(exact), one, none)
        values = add_pieces(
            jnp.dot(left, chosen.astype(jnp.bfloat16), preferred_element_type=jnp.float32)
        )
        out[b : b + 1, :] = jnp.sum(
            jnp.where(lane == places % half, values, 0.0), axis=0, keepdims=True
        )


def slab_body(perm, direction, resid, codes, pct, *refs, axis):
    *table, shuffled, sums = refs
    rhs = direction.shape[0]
    slab = codes.shape[1]
    table = jnp.concatenate([block[...] for block in table], axis=0)
    shard = table.size // lax.axis_size(axis)
    lookup(table, perm[...] ^ (lax.axis_index(axis) * shard), shuffled)
    mean, scale = spread(pct[...])
    straight = direction[...]
    both = jnp.concatenate([straight, shuffled[...] * straight], axis=0)
    product = add_pieces(
        jnp.dot(bf16_pieces(both), codes[...], preferred_element_type=jnp.float32)
    )
    sums[:, :slab] = scale * (product - mean * jnp.sum(both, axis=1, keepdims=True))
    left = resid[...]
    norm = jnp.sum(left * left, axis=1, keepdims=True)
    length = jnp.sum(straight * straight, axis=1, keepdims=True)
    sums[:rhs, slab:] = jnp.broadcast_to(norm, (rhs, LANES))
    sums[rhs:, slab:] = jnp.broadcast_to(length, (rhs, LANES))


def slab_sums(table, perm, direction, resid, codes, pct, axis):
    rhs, slab = direction.shape[0], codes.shape[1]
    return call(
        functools.partial(slab_body, axis=axis),
        [in_vmem(perm.shape), in_vmem((2 * rhs, slab + LANES))],
        [WHOLE] * (5 + len(table)),
    )(perm, direction, resid, codes, pct, *table)


def kernel_body(sums, flipped, pct, shuffled, var_comp, out, *, slab_total):
    rhs, count = shuffled.shape
    slab = flipped.shape[0]
    weights = sums[:, :slab]
    squares = jnp.sum(weights * weights, axis=1, keepdims=True)
    mean, scale = spread(pct[...])
    weights = scale * weights
    product = add_pieces(
        jnp.dot(bf16_pieces(weights), flipped[...], preferred_element_type=jnp.float32)
    ) - jnp.sum(mean * weights, axis=1, keepdims=True)
    share = 1.0 / slab_total
    out[:, :count] = (
        var_comp[1] * product[:rhs] + var_comp[2] * shuffled[...] * product[rhs:]
    ) * share
    energy = (var_comp[1] * squares[:rhs] + var_comp[2] * squares[rhs:]) * share
    out[:, count:] = jnp.broadcast_to(energy, (rhs, LANES))


def kernel_part(sums, flipped, pct, shuffled, var_comp, slab_total):
    rhs, count = shuffled.shape
    return call(
        functools.partial(kernel_body, slab_total=slab_total),
        in_vmem((rhs, count + LANES)),
        [WHOLE] * 4 + [SCALARS],
    )(sums, flipped, pct, shuffled, var_comp)


def step_body(applied, sums, shuffled, direction, resid, solution, codes, pct, empty, var_comp,
              new_solution, new_resid, scores, *, root):
    rhs, count = shuffled.shape
    tests = codes.shape[1]
    norms = sums[:, -LANES:]
    straight = direction[...]
    image = var_comp[0] * straight + applied[:, :count]
    curvature = var_comp[0] * norms[rhs:, :1] + applied[:, count : count + 1]
    alpha = norms[:rhs, :1] / curvature
    left = resid[...] - alpha * image
    new_resid[...] = left
    new_solution[...] = solution[...] + alpha * straight
    both = jnp.concatenate([left, shuffled[...] * left], axis=0)
    mean, scale = spread(pct[...])
    product = add_pieces(
        jnp.dot(bf16_pieces(both), codes[...], preferred_element_type=jnp.float32)
    )
    scores[:, :tests] = (scale / root) * (product - mean * jnp.sum(both, axis=1, keepdims=True))
    norm = jnp.sum(left * left, axis=1, keepdims=True)
    scores[:rhs, tests:] = jnp.broadcast_to(norm, (rhs, LANES))
    scores[rhs:, tests:] = empty[...]


def step(applied, sums, shuffled, direction, resid, solution, codes, pct, empty, var_comp, root):
    rhs, count = shuffled.shape
    return call(
        functools.partial(step_body, root=root),
        [
            in_vmem((rhs, count)),
            in_vmem((rhs, count)),
            in_vmem((2 * rhs, codes.shape[1] + LANES)),
        ],
        [WHOLE] * 9 + [SCALARS],
    )(applied, sums, shuffled, direction, resid, solution, codes, pct, empty, var_comp)


def finish_body(sums, new_resid, direction, *refs):
    *parts, new_direction, scores = refs
    rhs = direction.shape[0]
    tests = scores.shape[1]
    total = add_parts([part[...] for part in parts])
    scores[...] = total[:, :tests]
    ratio = total[:rhs, tests : tests + 1] / sums[:rhs, -LANES:][:, :1]
    new_direction[...] = new_resid[...] + ratio * direction[...]


def finish(parts, sums, new_resid, direction):
    rows, columns = parts[0].shape
    return call(
        finish_body,
        [
            jax.ShapeDtypeStruct(direction.shape, jnp.float32),
            jax.ShapeDtypeStruct((rows, columns - LANES), jnp.float32),
        ],
        [WHOLE] * (3 + len(parts)),
    )(sums, new_resid, direction, *parts)


def swap(x, axis, distance):
    size = lax.axis_size(axis)
    return lax.ppermute(x, axis, [(i, i ^ distance) for i in range(size)])


def add_parts(parts):
    if len(parts) == 4:
        return (parts[0] + parts[1]) + (parts[2] + parts[3])
    return sum(parts[1:], parts[0])


def sum_parts(x, axis, widths, unit=1):
    parts = [x]
    for width in widths(lax.axis_size(axis) // unit):
        held = add_parts(parts)
        parts = [held] + [swap(held, axis, k * unit) for k in range(1, width)]
        unit *= width
    return parts


def sum_all(x, axis, widths, unit=1):
    return add_parts(sum_parts(x, axis, widths, unit))


def gather_all(x, axis, widths):
    blocks = [x]
    unit = 1
    for width in widths(lax.axis_size(axis)):
        held = blocks[0] if len(blocks) == 1 else stack(blocks)
        blocks = [held] + [swap(held, axis, k * unit) for k in range(1, width)]
        unit *= width
    return blocks


def pairs_then_fours(size):
    bits = size.bit_length() - 1
    return [2] * (bits % 2) + [4] * (bits // 2)


def pairs(size):
    return [2] * (size.bit_length() - 1)


def local(
    geno, allele_pct, test_geno, test_pct, exposure, perm, var_comp, solution, resid, direction
):
    rhs, count = resid.shape
    slab = geno.shape[1]
    tests = test_geno.shape[1]
    slab_total = float(slab * lax.axis_size("var"))
    root = math.sqrt(count * lax.axis_size("samp"))
    pct = allele_pct.reshape(1, slab)
    empty, shard = lax.optimization_barrier((blank(rhs), exposure.reshape(-1, LANES)))
    table = gather_all(shard, "samp", pairs_then_fours)
    codes = cast_codes(geno)
    shuffled, sums = slab_sums(table, perm, direction, resid, codes, pct, "samp")
    sums = sums + swap(sums, "samp", 1)
    codes, sums = lax.optimization_barrier((codes, sums))
    flipped = flip_codes(codes, 0, slab)
    sums = sum_all(sums, "samp", pairs_then_fours, 2)
    applied = kernel_part(sums, flipped, pct, shuffled, var_comp, slab_total)
    applied = sum_all(applied, "var", pairs)
    test_codes = cast_codes(test_geno)
    new_solution, new_resid, scores = step(
        applied, sums, shuffled, direction, resid, solution, test_codes,
        test_pct.reshape(1, tests), empty, var_comp, root,
    )
    parts = sum_parts(scores, "samp", pairs_then_fours)
    new_direction, scores = finish(parts, sums, new_resid, direction)
    return (new_solution, new_resid, new_direction, scores)


def solution(mesh):
    return jax.shard_map(
        local,
        mesh=mesh,
        in_specs=(
            P("samp", "var"),
            P("var"),
            P("samp", "var"),
            P("var"),
            P("samp"),
            P(None, "samp"),
            P(),
            P(None, "samp"),
            P(None, "samp"),
            P(None, "samp"),
        ),
        out_specs=(P(None, "samp"), P(None, "samp"), P(None, "samp"), P(None, "var")),
        check_vma=False,
    )
```

```python
import functools
import math

import jax
import jax.numpy as jnp
from jax import lax
from jax.experimental import pallas as pl
from jax.experimental.pallas import tpu as pltpu
from jax.sharding import PartitionSpec as P

LANES = 128
CAST_ROWS = 64
FLIP_ROWS = 512
VMEM_BYTES = 10 << 20
WHOLE = pl.BlockSpec(memory_space=pltpu.VMEM)
SCALARS = pl.BlockSpec(memory_space=pltpu.SMEM)
GATHER_ORDER = (3, 2, 1)
SLAB_ORDER = (2, 1, 3)
SCORE_ORDER = (3, 1, 2)


def in_vmem(shape, dtype=jnp.float32):
    return pltpu.VMEM(shape, dtype)


def call(body, out_shape, in_specs, **kwargs):
    return pl.pallas_call(
        body,
        out_shape=out_shape,
        in_specs=in_specs,
        out_specs=jax.tree.map(lambda _: WHOLE, out_shape),
        compiler_params=pltpu.CompilerParams(vmem_limit_bytes=VMEM_BYTES),
        **kwargs,
    )


def cost(products):
    return pl.CostEstimate(flops=8 * products, bytes_accessed=0, transcendentals=0)


def bf16_pieces(x):
    pieces = []
    for _ in range(3):
        piece = x.astype(jnp.bfloat16)
        pieces.append(piece)
        x = x - piece.astype(jnp.float32)
    return jnp.concatenate(pieces, axis=0)


def add_pieces(y):
    rows = y.shape[0] // 3
    return y[:rows] + y[rows : 2 * rows] + y[2 * rows :]


def spread(pct):
    freq = pct.astype(jnp.float32) / 100.0
    return 2.0 * freq, lax.rsqrt(2.0 * freq * (1.0 - freq))


def cast_body(geno, codes):
    rows = math.gcd(geno.shape[0], CAST_ROWS)

    @pl.loop(0, geno.shape[0] // rows)
    def _(step):
        here = pl.ds(pl.multiple_of(step * rows, rows), rows)
        codes[here, :] = geno[here, :].astype(jnp.float32).astype(jnp.bfloat16)


def cast_codes(geno):
    return call(cast_body, in_vmem(geno.shape, jnp.bfloat16), [WHOLE])(geno)


def flip_body(codes, flipped, *, start):
    rows = math.gcd(codes.shape[0], FLIP_ROWS)
    columns = slice(start, start + flipped.shape[0])

    @pl.loop(0, codes.shape[0] // rows)
    def _(step):
        here = pl.ds(pl.multiple_of(step * rows, rows), rows)
        flipped[:, here] = codes[here, columns].T


def flip_codes(codes, start, width):
    return call(
        functools.partial(flip_body, start=start),
        in_vmem((width, codes.shape[0]), codes.dtype),
        [WHOLE],
        cost_estimate=cost(64 * codes.shape[0] * width),
    )(codes)


def blank_body(out):
    out[...] = jnp.zeros_like(out)


def blank(rows):
    early = pl.CostEstimate(flops=1 << 34, bytes_accessed=1 << 25, transcendentals=0)
    return call(blank_body, in_vmem((rows, LANES)), [], cost_estimate=early)()


def stack_body(*refs):
    *blocks, out = refs
    out[...] = jnp.concatenate([block[...] for block in blocks], axis=0)


def stack(blocks):
    rows = sum(block.shape[0] for block in blocks)
    return call(stack_body, in_vmem((rows, LANES)), [WHOLE] * len(blocks))(*blocks)


def lookup(table, index, out):
    height = table.shape[0]
    rhs, count = index.shape
    half = LANES // 2
    exact = jnp.bfloat16 if 2 * height <= 256 else jnp.float32
    row = lax.broadcasted_iota(jnp.int32, (2 * height, count), 0).astype(exact)
    lane = lax.broadcasted_iota(jnp.int32, (half, count), 0)
    halves = table.T
    left = bf16_pieces(jnp.concatenate([halves[:half], halves[half:]], axis=1))
    one, none = jnp.ones((), exact), jnp.zeros((), exact)
    for b in range(rhs):
        places = index[b : b + 1, :]
        wanted = places // LANES + height * (places // half % 2)
        chosen = jnp.where(row == wanted.astype(jnp.float32).astype(exact), one, none)
        values = add_pieces(
            jnp.dot(left, chosen.astype(jnp.bfloat16), preferred_element_type=jnp.float32)
        )
        out[b : b + 1, :] = jnp.sum(
            jnp.where(lane == places % half, values, 0.0), axis=0, keepdims=True
        )


def slab_body(perm, direction, resid, codes, pct, *refs, axis):
    *table, shuffled, sums = refs
    rhs = direction.shape[0]
    slab = codes.shape[1]
    table = jnp.concatenate([block[...] for block in by_distance(table, GATHER_ORDER)], axis=0)
    shard = table.size // lax.axis_size(axis)
    lookup(table, perm[...] ^ (lax.axis_index(axis) * shard), shuffled)
    mean, scale = spread(pct[...])
    straight = direction[...]
    both = jnp.concatenate([straight, shuffled[...] * straight], axis=0)
    product = add_pieces(
        jnp.dot(bf16_pieces(both), codes[...], preferred_element_type=jnp.float32)
    )
    sums[:, :slab] = scale * (product - mean * jnp.sum(both, axis=1, keepdims=True))
    left = resid[...]
    norm = jnp.sum(left * left, axis=1, keepdims=True)
    length = jnp.sum(straight * straight, axis=1, keepdims=True)
    sums[:rhs, slab:] = jnp.broadcast_to(norm, (rhs, LANES))
    sums[rhs:, slab:] = jnp.broadcast_to(length, (rhs, LANES))


def slab_sums(table, perm, direction, resid, codes, pct, axis):
    rhs, slab = direction.shape[0], codes.shape[1]
    return call(
        functools.partial(slab_body, axis=axis),
        [in_vmem(perm.shape), in_vmem((2 * rhs, slab + LANES))],
        [WHOLE] * (5 + len(table)),
    )(perm, direction, resid, codes, pct, *table)


def kernel_body(sums, flipped, pct, shuffled, var_comp, out, *, slab_total):
    rhs, count = shuffled.shape
    slab = flipped.shape[0]
    weights = sums[:, :slab]
    squares = jnp.sum(weights * weights, axis=1, keepdims=True)
    mean, scale = spread(pct[...])
    weights = scale * weights
    product = add_pieces(
        jnp.dot(bf16_pieces(weights), flipped[...], preferred_element_type=jnp.float32)
    ) - jnp.sum(mean * weights, axis=1, keepdims=True)
    share = 1.0 / slab_total
    out[:, :count] = (
        var_comp[1] * product[:rhs] + var_comp[2] * shuffled[...] * product[rhs:]
    ) * share
    energy = (var_comp[1] * squares[:rhs] + var_comp[2] * squares[rhs:]) * share
    out[:, count:] = jnp.broadcast_to(energy, (rhs, LANES))


def kernel_part(sums, flipped, pct, shuffled, var_comp, slab_total):
    rhs, count = shuffled.shape
    return call(
        functools.partial(kernel_body, slab_total=slab_total),
        in_vmem((rhs, count + LANES)),
        [WHOLE] * 4 + [SCALARS],
    )(sums, flipped, pct, shuffled, var_comp)


def step_body(applied, sums, shuffled, direction, resid, solution, codes, pct, empty, var_comp,
              new_solution, new_resid, scores, *, root):
    rhs, count = shuffled.shape
    tests = codes.shape[1]
    norms = sums[:, -LANES:]
    straight = direction[...]
    image = var_comp[0] * straight + applied[:, :count]
    curvature = var_comp[0] * norms[rhs:, :1] + applied[:, count : count + 1]
    alpha = norms[:rhs, :1] / curvature
    left = resid[...] - alpha * image
    new_resid[...] = left
    new_solution[...] = solution[...] + alpha * straight
    both = jnp.concatenate([left, shuffled[...] * left], axis=0)
    mean, scale = spread(pct[...])
    product = add_pieces(
        jnp.dot(bf16_pieces(both), codes[...], preferred_element_type=jnp.float32)
    )
    scores[:, :tests] = (scale / root) * (product - mean * jnp.sum(both, axis=1, keepdims=True))
    norm = jnp.sum(left * left, axis=1, keepdims=True)
    scores[:rhs, tests:] = jnp.broadcast_to(norm, (rhs, LANES))
    scores[rhs:, tests:] = empty[...]


def step(applied, sums, shuffled, direction, resid, solution, codes, pct, empty, var_comp, root):
    rhs, count = shuffled.shape
    return call(
        functools.partial(step_body, root=root),
        [
            in_vmem((rhs, count)),
            in_vmem((rhs, count)),
            in_vmem((2 * rhs, codes.shape[1] + LANES)),
        ],
        [WHOLE] * 9 + [SCALARS],
    )(applied, sums, shuffled, direction, resid, solution, codes, pct, empty, var_comp)


def finish_body(sums, new_resid, direction, *refs):
    *parts, new_direction, scores = refs
    rhs = direction.shape[0]
    tests = scores.shape[1]
    total = add_parts([part[...] for part in by_distance(parts, SCORE_ORDER)])
    scores[...] = total[:, :tests]
    ratio = total[:rhs, tests : tests + 1] / sums[:rhs, -LANES:][:, :1]
    new_direction[...] = new_resid[...] + ratio * direction[...]


def finish(parts, sums, new_resid, direction):
    rows, columns = parts[0].shape
    return call(
        finish_body,
        [
            jax.ShapeDtypeStruct(direction.shape, jnp.float32),
            jax.ShapeDtypeStruct((rows, columns - LANES), jnp.float32),
        ],
        [WHOLE] * (3 + len(parts)),
    )(sums, new_resid, direction, *parts)


def add_body(*refs):
    *parts, out = refs
    out[...] = add_parts([part[...] for part in by_distance(parts, SLAB_ORDER)])


def add_up(parts):
    return call(add_body, in_vmem(parts[0].shape), [WHOLE] * len(parts))(*parts)


def swap(x, axis, distance):
    size = lax.axis_size(axis)
    return lax.ppermute(x, axis, [(i, i ^ distance) for i in range(size)])


def swaps(x, axis, width, unit, order):
    return [swap(x, axis, k * unit) for k in order if k < width]


def by_distance(parts, order):
    order = [k for k in order if k < len(parts)]
    return [parts[0]] + [parts[1 + order.index(k)] for k in range(1, len(parts))]


def add_parts(parts):
    if len(parts) == 4:
        return (parts[0] + parts[1]) + (parts[2] + parts[3])
    return sum(parts[1:], parts[0])


def sum_parts(x, axis, widths, order, unit=1):
    parts = [x]
    for width in widths(lax.axis_size(axis) // unit):
        held = add_parts(by_distance(parts, order))
        parts = [held] + swaps(held, axis, width, unit, order)
        unit *= width
    return parts


def sum_all(x, axis, widths):
    return add_parts(by_distance(sum_parts(x, axis, widths, (1,)), (1,)))


def gather_all(x, axis, widths):
    blocks = [x]
    unit = 1
    for width in widths(lax.axis_size(axis)):
        held = blocks[0] if len(blocks) == 1 else stack(by_distance(blocks, GATHER_ORDER))
        blocks = [held] + swaps(held, axis, width, unit, GATHER_ORDER)
        unit *= width
    return blocks


def pairs_then_fours(size):
    bits = size.bit_length() - 1
    return [2] * (bits % 2) + [4] * (bits // 2)


def pairs(size):
    return [2] * (size.bit_length() - 1)


def local(
    geno, allele_pct, test_geno, test_pct, exposure, perm, var_comp, solution, resid, direction
):
    rhs, count = resid.shape
    slab = geno.shape[1]
    tests = test_geno.shape[1]
    slab_total = float(slab * lax.axis_size("var"))
    root = math.sqrt(count * lax.axis_size("samp"))
    pct = allele_pct.reshape(1, slab)
    empty, shard = lax.optimization_barrier((blank(rhs), exposure.reshape(-1, LANES)))
    table = gather_all(shard, "samp", pairs_then_fours)
    codes = cast_codes(geno)
    shuffled, sums = slab_sums(table, perm, direction, resid, codes, pct, "samp")
    sums = sums + swap(sums, "samp", 1)
    codes, sums = lax.optimization_barrier((codes, sums))
    flipped = flip_codes(codes, 0, slab)
    parts = sum_parts(sums, "samp", pairs_then_fours, SLAB_ORDER, 2)
    sums = add_up(parts)
    applied = kernel_part(sums, flipped, pct, shuffled, var_comp, slab_total)
    applied = sum_all(applied, "var", pairs)
    test_codes = cast_codes(test_geno)
    new_solution, new_resid, scores = step(
        applied, sums, shuffled, direction, resid, solution, test_codes,
        test_pct.reshape(1, tests), empty, var_comp, root,
    )
    parts = sum_parts(scores, "samp", pairs_then_fours, SCORE_ORDER)
    new_direction, scores = finish(parts, sums, new_resid, direction)
    return (new_solution, new_resid, new_direction, scores)


def solution(mesh):
    return jax.shard_map(
        local,
        mesh=mesh,
        in_specs=(
            P("samp", "var"),
            P("var"),
            P("samp", "var"),
            P("var"),
            P("samp"),
            P(None, "samp"),
            P(),
            P(None, "samp"),
            P(None, "samp"),
            P(None, "samp"),
        ),
        out_specs=(P(None, "samp"), P(None, "samp"), P(None, "samp"), P(None, "var")),
        check_vma=False,
    )
```

```python
import functools
import math

import jax
import jax.numpy as jnp
from jax import lax
from jax.experimental import pallas as pl
from jax.experimental.pallas import tpu as pltpu
from jax.sharding import PartitionSpec as P

LANES = 128
CAST_ROWS = 64
FLIP_ROWS = 512
VMEM_BYTES = 10 << 20
WHOLE = pl.BlockSpec(memory_space=pltpu.VMEM)
SCALARS = pl.BlockSpec(memory_space=pltpu.SMEM)
GATHER_ORDER = (3, 2, 1)
SLAB_ORDER = (2, 1, 3)
SCORE_ORDER = (3, 1, 2)


def in_vmem(shape, dtype=jnp.float32):
    return pltpu.VMEM(shape, dtype)


def call(body, out_shape, in_specs, **kwargs):
    return pl.pallas_call(
        body,
        out_shape=out_shape,
        in_specs=in_specs,
        out_specs=jax.tree.map(lambda _: WHOLE, out_shape),
        compiler_params=pltpu.CompilerParams(vmem_limit_bytes=VMEM_BYTES),
        **kwargs,
    )


def cost(products):
    return pl.CostEstimate(flops=8 * products, bytes_accessed=0, transcendentals=0)


def bf16_pieces(x):
    pieces = []
    for _ in range(3):
        piece = x.astype(jnp.bfloat16)
        pieces.append(piece)
        x = x - piece.astype(jnp.float32)
    return jnp.concatenate(pieces, axis=0)


def add_pieces(y):
    rows = y.shape[0] // 3
    return y[:rows] + y[rows : 2 * rows] + y[2 * rows :]


def spread(pct):
    freq = pct.astype(jnp.float32) / 100.0
    return 2.0 * freq, lax.rsqrt(2.0 * freq * (1.0 - freq))


def cast_body(geno, codes):
    rows = math.gcd(geno.shape[0], CAST_ROWS)

    @pl.loop(0, geno.shape[0] // rows)
    def _(step):
        here = pl.ds(pl.multiple_of(step * rows, rows), rows)
        codes[here, :] = geno[here, :].astype(jnp.float32).astype(jnp.bfloat16)


def cast_codes(geno):
    return call(cast_body, in_vmem(geno.shape, jnp.bfloat16), [WHOLE])(geno)


def flip_body(codes, flipped, *, start):
    rows = math.gcd(codes.shape[0], FLIP_ROWS)
    columns = slice(start, start + flipped.shape[0])

    @pl.loop(0, codes.shape[0] // rows)
    def _(step):
        here = pl.ds(pl.multiple_of(step * rows, rows), rows)
        flipped[:, here] = codes[here, columns].T


def flip_codes(codes, start, width):
    return call(
        functools.partial(flip_body, start=start),
        in_vmem((width, codes.shape[0]), codes.dtype),
        [WHOLE],
        cost_estimate=cost(64 * codes.shape[0] * width),
    )(codes)


def blank_body(out):
    out[...] = jnp.zeros_like(out)


def blank(rows):
    early = pl.CostEstimate(flops=1 << 34, bytes_accessed=1 << 25, transcendentals=0)
    return call(blank_body, in_vmem((rows, LANES)), [], cost_estimate=early)()


def stack_body(*refs):
    *blocks, out = refs
    out[...] = jnp.concatenate([block[...] for block in blocks], axis=0)


def stack(blocks):
    rows = sum(block.shape[0] for block in blocks)
    return call(stack_body, in_vmem((rows, LANES)), [WHOLE] * len(blocks))(*blocks)


def lookup(table, index, out):
    height = table.shape[0]
    rhs, count = index.shape
    half = LANES // 2
    exact = jnp.bfloat16 if 2 * height <= 256 else jnp.float32
    row = lax.broadcasted_iota(jnp.int32, (2 * height, count), 0).astype(exact)
    lane = lax.broadcasted_iota(jnp.int32, (half, count), 0)
    halves = table.T
    left = bf16_pieces(jnp.concatenate([halves[:half], halves[half:]], axis=1))
    one, none = jnp.ones((), exact), jnp.zeros((), exact)
    for b in range(rhs):
        places = index[b : b + 1, :]
        wanted = places // LANES + height * (places // half % 2)
        chosen = jnp.where(row == wanted.astype(jnp.float32).astype(exact), one, none)
        values = add_pieces(
            jnp.dot(left, chosen.astype(jnp.bfloat16), preferred_element_type=jnp.float32)
        )
        out[b : b + 1, :] = jnp.sum(
            jnp.where(lane == places % half, values, 0.0), axis=0, keepdims=True
        )


def slab_body(perm, direction, resid, codes, pct, *refs, axis):
    *table, shuffled, sums = refs
    rhs = direction.shape[0]
    slab = codes.shape[1]
    table = jnp.concatenate([block[...] for block in by_distance(table, GATHER_ORDER)], axis=0)
    shard = table.size // lax.axis_size(axis)
    lookup(table, perm[...] ^ (lax.axis_index(axis) * shard), shuffled)
    mean, scale = spread(pct[...])
    straight = direction[...]
    both = jnp.concatenate([straight, shuffled[...] * straight], axis=0)
    product = add_pieces(
        jnp.dot(bf16_pieces(both), codes[...], preferred_element_type=jnp.float32)
    )
    sums[:, :slab] = scale * (product - mean * jnp.sum(both, axis=1, keepdims=True))
    left = resid[...]
    norm = jnp.sum(left * left, axis=1, keepdims=True)
    length = jnp.sum(straight * straight, axis=1, keepdims=True)
    sums[:rhs, slab:] = jnp.broadcast_to(norm, (rhs, LANES))
    sums[rhs:, slab:] = jnp.broadcast_to(length, (rhs, LANES))


def slab_sums(table, perm, direction, resid, codes, pct, axis):
    rhs, slab = direction.shape[0], codes.shape[1]
    return call(
        functools.partial(slab_body, axis=axis),
        [in_vmem(perm.shape), in_vmem((2 * rhs, slab + LANES))],
        [WHOLE] * (5 + len(table)),
    )(perm, direction, resid, codes, pct, *table)


def kernel_body(sums, flipped, pct, shuffled, var_comp, out, *, slab_total):
    rhs, count = shuffled.shape
    slab = flipped.shape[0]
    weights = sums[:, :slab]
    squares = jnp.sum(weights * weights, axis=1, keepdims=True)
    mean, scale = spread(pct[...])
    weights = scale * weights
    product = add_pieces(
        jnp.dot(bf16_pieces(weights), flipped[...], preferred_element_type=jnp.float32)
    ) - jnp.sum(mean * weights, axis=1, keepdims=True)
    share = 1.0 / slab_total
    out[:, :count] = (
        var_comp[1] * product[:rhs] + var_comp[2] * shuffled[...] * product[rhs:]
    ) * share
    energy = (var_comp[1] * squares[:rhs] + var_comp[2] * squares[rhs:]) * share
    out[:, count:] = jnp.broadcast_to(energy, (rhs, LANES))


def kernel_part(sums, flipped, pct, shuffled, var_comp, slab_total):
    rhs, count = shuffled.shape
    return call(
        functools.partial(kernel_body, slab_total=slab_total),
        in_vmem((rhs, count + LANES)),
        [WHOLE] * 4 + [SCALARS],
    )(sums, flipped, pct, shuffled, var_comp)


def step_body(applied, sums, shuffled, direction, resid, solution, codes, pct, empty, var_comp,
              new_solution, new_resid, scores, *, root):
    rhs, count = shuffled.shape
    tests = codes.shape[1]
    norms = sums[:, -LANES:]
    straight = direction[...]
    image = var_comp[0] * straight + applied[:, :count]
    curvature = var_comp[0] * norms[rhs:, :1] + applied[:, count : count + 1]
    alpha = norms[:rhs, :1] / curvature
    left = resid[...] - alpha * image
    new_resid[...] = left
    new_solution[...] = solution[...] + alpha * straight
    both = jnp.concatenate([left, shuffled[...] * left], axis=0)
    mean, scale = spread(pct[...])
    product = add_pieces(
        jnp.dot(bf16_pieces(both), codes[...], preferred_element_type=jnp.float32)
    )
    scores[:, :tests] = (scale / root) * (product - mean * jnp.sum(both, axis=1, keepdims=True))
    norm = jnp.sum(left * left, axis=1, keepdims=True)
    scores[:rhs, tests:] = jnp.broadcast_to(norm, (rhs, LANES))
    scores[rhs:, tests:] = empty[...]


def step(applied, sums, shuffled, direction, resid, solution, codes, pct, empty, var_comp, root):
    rhs, count = shuffled.shape
    return call(
        functools.partial(step_body, root=root),
        [
            in_vmem((rhs, count)),
            in_vmem((rhs, count)),
            in_vmem((2 * rhs, codes.shape[1] + LANES)),
        ],
        [WHOLE] * 9 + [SCALARS],
    )(applied, sums, shuffled, direction, resid, solution, codes, pct, empty, var_comp)


def finish_body(sums, new_resid, direction, *refs):
    *parts, new_direction, scores = refs
    rhs = direction.shape[0]
    tests = scores.shape[1]
    total = add_parts([part[...] for part in by_distance(parts, SCORE_ORDER)])
    scores[...] = total[:, :tests]
    ratio = total[:rhs, tests : tests + 1] / sums[:rhs, -LANES:][:, :1]
    new_direction[...] = new_resid[...] + ratio * direction[...]


def finish(parts, sums, new_resid, direction):
    rows, columns = parts[0].shape
    return call(
        finish_body,
        [
            jax.ShapeDtypeStruct(direction.shape, jnp.float32),
            jax.ShapeDtypeStruct((rows, columns - LANES), jnp.float32),
        ],
        [WHOLE] * (3 + len(parts)),
    )(sums, new_resid, direction, *parts)


def add_body(*refs):
    *parts, out = refs
    out[...] = add_parts([part[...] for part in by_distance(parts, SLAB_ORDER)])


def add_up(parts):
    return call(add_body, in_vmem(parts[0].shape), [WHOLE] * len(parts))(*parts)


def swap(x, axis, distance):
    size = lax.axis_size(axis)
    return lax.ppermute(x, axis, [(i, i ^ distance) for i in range(size)])


def swaps(x, axis, width, unit, order):
    return [swap(x, axis, k * unit) for k in order if k < width]


def by_distance(parts, order):
    order = [k for k in order if k < len(parts)]
    return [parts[0]] + [parts[1 + order.index(k)] for k in range(1, len(parts))]


def add_parts(parts):
    if len(parts) == 4:
        return (parts[0] + parts[1]) + (parts[2] + parts[3])
    return sum(parts[1:], parts[0])


def sum_parts(x, axis, widths, order, unit=1):
    parts = [x]
    for width in widths(lax.axis_size(axis) // unit):
        held = add_parts(by_distance(parts, order))
        parts = [held] + swaps(held, axis, width, unit, order)
        unit *= width
    return parts


def sum_all(x, axis, widths):
    return add_parts(by_distance(sum_parts(x, axis, widths, (1,)), (1,)))


def gather_all(x, axis, widths, beside):
    blocks = [x]
    unit = 1
    for width in widths(lax.axis_size(axis)):
        held = blocks[0] if len(blocks) == 1 else stack(by_distance(blocks, GATHER_ORDER))
        blocks = [held] + swaps(held, axis, width, unit, GATHER_ORDER)
        if unit == 1:
            beside, blocks[1] = lax.optimization_barrier((beside, blocks[1]))
        unit *= width
    return blocks, beside


def pairs_then_fours(size):
    bits = size.bit_length() - 1
    return [2] * (bits % 2) + [4] * (bits // 2)


def pairs(size):
    return [2] * (size.bit_length() - 1)


def local(
    geno, allele_pct, test_geno, test_pct, exposure, perm, var_comp, solution, resid, direction
):
    rhs, count = resid.shape
    slab = geno.shape[1]
    tests = test_geno.shape[1]
    slab_total = float(slab * lax.axis_size("var"))
    root = math.sqrt(count * lax.axis_size("samp"))
    pct = allele_pct.reshape(1, slab)
    table, empty = gather_all(
        exposure.reshape(-1, LANES), "samp", pairs_then_fours, blank(rhs)
    )
    codes = cast_codes(geno)
    shuffled, sums = slab_sums(table, perm, direction, resid, codes, pct, "samp")
    sums = sums + swap(sums, "samp", 1)
    codes, sums = lax.optimization_barrier((codes, sums))
    flipped = flip_codes(codes, 0, slab)
    parts = sum_parts(sums, "samp", pairs_then_fours, SLAB_ORDER, 2)
    sums = add_up(parts)
    applied = kernel_part(sums, flipped, pct, shuffled, var_comp, slab_total)
    applied = sum_all(applied, "var", pairs)
    test_codes = cast_codes(test_geno)
    new_solution, new_resid, scores = step(
        applied, sums, shuffled, direction, resid, solution, test_codes,
        test_pct.reshape(1, tests), empty, var_comp, root,
    )
    parts = sum_parts(scores, "samp", pairs_then_fours, SCORE_ORDER)
    new_direction, scores = finish(parts, sums, new_resid, direction)
    return (new_solution, new_resid, new_direction, scores)


def solution(mesh):
    return jax.shard_map(
        local,
        mesh=mesh,
        in_specs=(
            P("samp", "var"),
            P("var"),
            P("samp", "var"),
            P("var"),
            P("samp"),
            P(None, "samp"),
            P(),
            P(None, "samp"),
            P(None, "samp"),
            P(None, "samp"),
        ),
        out_specs=(P(None, "samp"), P(None, "samp"), P(None, "samp"), P(None, "var")),
        check_vma=False,
    )
```

```python
import functools
import math

import jax
import jax.numpy as jnp
from jax import lax
from jax.experimental import pallas as pl
from jax.experimental.pallas import tpu as pltpu
from jax.sharding import PartitionSpec as P

LANES = 128
CAST_ROWS = 64
FLIP_ROWS = 512
VMEM_BYTES = 10 << 20
WHOLE = pl.BlockSpec(memory_space=pltpu.VMEM)
SCALARS = pl.BlockSpec(memory_space=pltpu.SMEM)
GATHER_ORDER = (3, 2, 1)
SLAB_ORDER = (2, 1, 3)
SCORE_ORDER = (3, 2, 1)


def in_vmem(shape, dtype=jnp.float32):
    return pltpu.VMEM(shape, dtype)


def call(body, out_shape, in_specs, **kwargs):
    return pl.pallas_call(
        body,
        out_shape=out_shape,
        in_specs=in_specs,
        out_specs=jax.tree.map(lambda _: WHOLE, out_shape),
        compiler_params=pltpu.CompilerParams(vmem_limit_bytes=VMEM_BYTES),
        **kwargs,
    )


def cost(products):
    return pl.CostEstimate(flops=8 * products, bytes_accessed=0, transcendentals=0)


def bf16_pieces(x):
    pieces = []
    for _ in range(3):
        piece = x.astype(jnp.bfloat16)
        pieces.append(piece)
        x = x - piece.astype(jnp.float32)
    return jnp.concatenate(pieces, axis=0)


def add_pieces(y):
    rows = y.shape[0] // 3
    return y[:rows] + y[rows : 2 * rows] + y[2 * rows :]


def fold(x):
    return jnp.concatenate(
        [x[:, start : start + LANES] for start in range(0, x.shape[1], LANES)], axis=0
    )


def unfold(x, rows):
    return jnp.concatenate(
        [x[start : start + rows] for start in range(0, x.shape[0], rows)], axis=1
    )


def spread(pct):
    freq = pct.astype(jnp.float32) / 100.0
    return 2.0 * freq, lax.rsqrt(2.0 * freq * (1.0 - freq))


def cast_body(geno, codes):
    rows = math.gcd(geno.shape[0], CAST_ROWS)

    @pl.loop(0, geno.shape[0] // rows)
    def _(step):
        here = pl.ds(pl.multiple_of(step * rows, rows), rows)
        codes[here, :] = geno[here, :].astype(jnp.float32).astype(jnp.bfloat16)


def cast_codes(geno):
    return call(cast_body, in_vmem(geno.shape, jnp.bfloat16), [WHOLE])(geno)


def flip_body(codes, flipped, *, start):
    rows = math.gcd(codes.shape[0], FLIP_ROWS)
    columns = slice(start, start + flipped.shape[0])

    @pl.loop(0, codes.shape[0] // rows)
    def _(step):
        here = pl.ds(pl.multiple_of(step * rows, rows), rows)
        flipped[:, here] = codes[here, columns].T


def flip_codes(codes, start, width):
    return call(
        functools.partial(flip_body, start=start),
        in_vmem((width, codes.shape[0]), codes.dtype),
        [WHOLE],
        cost_estimate=cost(64 * codes.shape[0] * width),
    )(codes)


def blank_body(out):
    out[...] = jnp.zeros_like(out)


def blank(rows):
    early = pl.CostEstimate(flops=1 << 34, bytes_accessed=1 << 25, transcendentals=0)
    return call(blank_body, in_vmem((rows, LANES)), [], cost_estimate=early)()


def stack_body(*refs):
    *blocks, out = refs
    out[...] = jnp.concatenate([block[...] for block in blocks], axis=0)


def stack(blocks):
    rows = sum(block.shape[0] for block in blocks)
    return call(stack_body, in_vmem((rows, LANES)), [WHOLE] * len(blocks))(*blocks)


def lookup(table, index, out):
    height = table.shape[0]
    rhs, count = index.shape
    half = LANES // 2
    exact = jnp.bfloat16 if 2 * height <= 256 else jnp.float32
    row = lax.broadcasted_iota(jnp.int32, (2 * height, count), 0).astype(exact)
    lane = lax.broadcasted_iota(jnp.int32, (half, count), 0)
    halves = table.T
    left = bf16_pieces(jnp.concatenate([halves[:half], halves[half:]], axis=1))
    one, none = jnp.ones((), exact), jnp.zeros((), exact)
    for b in range(rhs):
        places = index[b : b + 1, :]
        wanted = places // LANES + height * (places // half % 2)
        chosen = jnp.where(row == wanted.astype(jnp.float32).astype(exact), one, none)
        values = add_pieces(
            jnp.dot(left, chosen.astype(jnp.bfloat16), preferred_element_type=jnp.float32)
        )
        out[b : b + 1, :] = jnp.sum(
            jnp.where(lane == places % half, values, 0.0), axis=0, keepdims=True
        )


def slab_body(perm, direction, resid, codes, pct, *refs, axis):
    *table, shuffled, sums = refs
    rhs = direction.shape[0]
    table = jnp.concatenate([block[...] for block in by_distance(table, GATHER_ORDER)], axis=0)
    shard = table.size // lax.axis_size(axis)
    lookup(table, perm[...] ^ (lax.axis_index(axis) * shard), shuffled)
    mean, scale = spread(pct[...])
    straight = direction[...]
    both = jnp.concatenate([straight, shuffled[...] * straight], axis=0)
    product = add_pieces(
        jnp.dot(bf16_pieces(both), codes[...], preferred_element_type=jnp.float32)
    )
    sums[:-rhs, :] = fold(scale * (product - mean * jnp.sum(both, axis=1, keepdims=True)))
    left = resid[...]
    norm = jnp.sum(left * left, axis=1, keepdims=True)
    length = jnp.sum(straight * straight, axis=1, keepdims=True)
    lane = lax.broadcasted_iota(jnp.int32, (rhs, LANES), 1)
    sums[-rhs:, :] = jnp.where(lane < LANES // 2, norm, length)


def slab_sums(table, perm, direction, resid, codes, pct, axis):
    rhs, slab = direction.shape[0], codes.shape[1]
    return call(
        functools.partial(slab_body, axis=axis),
        [in_vmem(perm.shape), in_vmem((2 * rhs * slab // LANES + rhs, LANES))],
        [WHOLE] * (5 + len(table)),
    )(perm, direction, resid, codes, pct, *table)


def kernel_body(sums, flipped, pct, shuffled, var_comp, out, *, slab_total):
    rhs, count = shuffled.shape
    weights = unfold(sums[:-rhs, :], 2 * rhs)
    squares = jnp.sum(weights * weights, axis=1, keepdims=True)
    mean, scale = spread(pct[...])
    weights = scale * weights
    product = add_pieces(
        jnp.dot(bf16_pieces(weights), flipped[...], preferred_element_type=jnp.float32)
    ) - jnp.sum(mean * weights, axis=1, keepdims=True)
    share = 1.0 / slab_total
    out[:, :count] = (
        var_comp[1] * product[:rhs] + var_comp[2] * shuffled[...] * product[rhs:]
    ) * share
    energy = (var_comp[1] * squares[:rhs] + var_comp[2] * squares[rhs:]) * share
    out[:, count:] = jnp.broadcast_to(energy, (rhs, LANES))


def kernel_part(sums, flipped, pct, shuffled, var_comp, slab_total):
    rhs, count = shuffled.shape
    return call(
        functools.partial(kernel_body, slab_total=slab_total),
        in_vmem((rhs, count + LANES)),
        [WHOLE] * 4 + [SCALARS],
    )(sums, flipped, pct, shuffled, var_comp)


def step_body(applied, sums, shuffled, direction, resid, solution, codes, pct, empty, var_comp,
              new_solution, new_resid, scores, *, root):
    rhs, count = shuffled.shape
    norms = sums[-rhs:, :]
    straight = direction[...]
    image = var_comp[0] * straight + applied[:, :count]
    curvature = var_comp[0] * norms[:, LANES // 2 : LANES // 2 + 1] + applied[:, count : count + 1]
    alpha = norms[:, :1] / curvature
    left = resid[...] - alpha * image
    new_resid[...] = left
    new_solution[...] = solution[...] + alpha * straight
    both = jnp.concatenate([left, shuffled[...] * left], axis=0)
    mean, scale = spread(pct[...])
    product = add_pieces(
        jnp.dot(bf16_pieces(both), codes[...], preferred_element_type=jnp.float32)
    )
    product -= mean * jnp.sum(both, axis=1, keepdims=True)
    scores[:-rhs, :] = fold((scale / root) * product)
    scores[-rhs:, :] = empty[...] + jnp.sum(left * left, axis=1, keepdims=True)


def step(applied, sums, shuffled, direction, resid, solution, codes, pct, empty, var_comp, root):
    rhs, count = shuffled.shape
    return call(
        functools.partial(step_body, root=root),
        [
            in_vmem((rhs, count)),
            in_vmem((rhs, count)),
            in_vmem((2 * rhs * codes.shape[1] // LANES + rhs, LANES)),
        ],
        [WHOLE] * 9 + [SCALARS],
    )(applied, sums, shuffled, direction, resid, solution, codes, pct, empty, var_comp)


def finish_body(sums, new_resid, direction, *refs):
    *parts, new_direction, scores = refs
    rhs = direction.shape[0]
    total = add_parts([part[...] for part in by_distance(parts, SCORE_ORDER)])
    scores[...] = unfold(total[:-rhs], 2 * rhs)
    ratio = total[-rhs:, :1] / sums[-rhs:, :1]
    new_direction[...] = new_resid[...] + ratio * direction[...]


def finish(parts, sums, new_resid, direction):
    rhs = direction.shape[0]
    tests = (parts[0].shape[0] - rhs) // (2 * rhs) * LANES
    return call(
        finish_body,
        [
            jax.ShapeDtypeStruct(direction.shape, jnp.float32),
            jax.ShapeDtypeStruct((2 * rhs, tests), jnp.float32),
        ],
        [WHOLE] * (3 + len(parts)),
    )(sums, new_resid, direction, *parts)


def add_body(*refs):
    *parts, out = refs
    out[...] = add_parts([part[...] for part in by_distance(parts, SLAB_ORDER)])


def add_up(parts):
    return call(add_body, in_vmem(parts[0].shape), [WHOLE] * len(parts))(*parts)


def swap(x, axis, distance):
    size = lax.axis_size(axis)
    return lax.ppermute(x, axis, [(i, i ^ distance) for i in range(size)])


def swaps(x, axis, width, unit, order):
    return [swap(x, axis, k * unit) for k in order if k < width]


def by_distance(parts, order):
    order = [k for k in order if k < len(parts)]
    return [parts[0]] + [parts[1 + order.index(k)] for k in range(1, len(parts))]


def add_parts(parts):
    if len(parts) == 4:
        return (parts[0] + parts[1]) + (parts[2] + parts[3])
    return sum(parts[1:], parts[0])


def sum_parts(x, axis, widths, order, unit=1):
    parts = [x]
    for width in widths(lax.axis_size(axis) // unit):
        held = add_parts(by_distance(parts, order))
        parts = [held] + swaps(held, axis, width, unit, order)
        unit *= width
    return parts


def sum_all(x, axis, widths):
    return add_parts(by_distance(sum_parts(x, axis, widths, (1,)), (1,)))


def gather_all(x, axis, widths, beside):
    blocks = [x]
    unit = 1
    for width in widths(lax.axis_size(axis)):
        held = blocks[0] if len(blocks) == 1 else stack(by_distance(blocks, GATHER_ORDER))
        blocks = [held] + swaps(held, axis, width, unit, GATHER_ORDER)
        if unit == 1:
            beside, blocks[1] = lax.optimization_barrier((beside, blocks[1]))
        unit *= width
    return blocks, beside


def pairs_then_fours(size):
    bits = size.bit_length() - 1
    return [2] * (bits % 2) + [4] * (bits // 2)


def pairs(size):
    return [2] * (size.bit_length() - 1)


def local(
    geno, allele_pct, test_geno, test_pct, exposure, perm, var_comp, solution, resid, direction
):
    rhs, count = resid.shape
    slab = geno.shape[1]
    tests = test_geno.shape[1]
    slab_total = float(slab * lax.axis_size("var"))
    root = math.sqrt(count * lax.axis_size("samp"))
    pct = allele_pct.reshape(1, slab)
    table, empty = gather_all(
        exposure.reshape(-1, LANES), "samp", pairs_then_fours, blank(rhs)
    )
    codes = cast_codes(geno)
    shuffled, sums = slab_sums(table, perm, direction, resid, codes, pct, "samp")
    sums = sums + swap(sums, "samp", 1)
    codes, sums = lax.optimization_barrier((codes, sums))
    flipped = flip_codes(codes, 0, slab)
    parts = sum_parts(sums, "samp", pairs_then_fours, SLAB_ORDER, 2)
    sums = add_up(parts)
    applied = kernel_part(sums, flipped, pct, shuffled, var_comp, slab_total)
    applied = sum_all(applied, "var", pairs)
    test_codes = cast_codes(test_geno)
    new_solution, new_resid, scores = step(
        applied, sums, shuffled, direction, resid, solution, test_codes,
        test_pct.reshape(1, tests), empty, var_comp, root,
    )
    parts = sum_parts(scores, "samp", pairs_then_fours, SCORE_ORDER)
    new_direction, scores = finish(parts, sums, new_resid, direction)
    return (new_solution, new_resid, new_direction, scores)


def solution(mesh):
    return jax.shard_map(
        local,
        mesh=mesh,
        in_specs=(
            P("samp", "var"),
            P("var"),
            P("samp", "var"),
            P("var"),
            P("samp"),
            P(None, "samp"),
            P(),
            P(None, "samp"),
            P(None, "samp"),
            P(None, "samp"),
        ),
        out_specs=(P(None, "samp"), P(None, "samp"), P(None, "samp"), P(None, "var")),
        check_vma=False,
    )
```

```python
import functools
import math

import jax
import jax.numpy as jnp
from jax import lax
from jax.experimental import pallas as pl
from jax.experimental.pallas import tpu as pltpu
from jax.sharding import PartitionSpec as P

LANES = 128
CAST_ROWS = 64
FLIP_ROWS = 512
VMEM_BYTES = 10 << 20
WHOLE = pl.BlockSpec(memory_space=pltpu.VMEM)
SCALARS = pl.BlockSpec(memory_space=pltpu.SMEM)
GATHER_ORDER = (3, 2, 1)
SLAB_ORDER = (2, 1, 3)
SCORE_ORDER = (3, 2, 1)


def in_vmem(shape, dtype=jnp.float32):
    return pltpu.VMEM(shape, dtype)


def call(body, out_shape, in_specs, **kwargs):
    return pl.pallas_call(
        body,
        out_shape=out_shape,
        in_specs=in_specs,
        out_specs=jax.tree.map(lambda _: WHOLE, out_shape),
        compiler_params=pltpu.CompilerParams(vmem_limit_bytes=VMEM_BYTES),
        **kwargs,
    )


def cost(products):
    return pl.CostEstimate(flops=8 * products, bytes_accessed=0, transcendentals=0)


def bf16_pieces(x):
    pieces = []
    for _ in range(3):
        piece = x.astype(jnp.bfloat16)
        pieces.append(piece)
        x = x - piece.astype(jnp.float32)
    return jnp.concatenate(pieces, axis=0)


def add_pieces(y):
    rows = y.shape[0] // 3
    return y[:rows] + y[rows : 2 * rows] + y[2 * rows :]


def fold(x, out):
    rows = x.shape[0]
    for block in range(x.shape[1] // LANES):
        out[block * rows : (block + 1) * rows, :] = x[:, block * LANES : (block + 1) * LANES]


def unfold(x, rows):
    return jnp.concatenate(
        [x[start : start + rows] for start in range(0, x.shape[0], rows)], axis=1
    )


def spread(pct):
    freq = pct.astype(jnp.float32) / 100.0
    return 2.0 * freq, lax.rsqrt(2.0 * freq * (1.0 - freq))


def cast_body(geno, codes):
    rows = math.gcd(geno.shape[0], CAST_ROWS)

    @pl.loop(0, geno.shape[0] // rows)
    def _(step):
        here = pl.ds(pl.multiple_of(step * rows, rows), rows)
        codes[here, :] = geno[here, :].astype(jnp.float32).astype(jnp.bfloat16)


def cast_codes(geno):
    return call(cast_body, in_vmem(geno.shape, jnp.bfloat16), [WHOLE])(geno)


def flip_body(codes, flipped, *, start):
    rows = math.gcd(codes.shape[0], FLIP_ROWS)
    columns = slice(start, start + flipped.shape[0])

    @pl.loop(0, codes.shape[0] // rows)
    def _(step):
        here = pl.ds(pl.multiple_of(step * rows, rows), rows)
        flipped[:, here] = codes[here, columns].T


def flip_codes(codes, start, width):
    return call(
        functools.partial(flip_body, start=start),
        in_vmem((width, codes.shape[0]), codes.dtype),
        [WHOLE],
        cost_estimate=cost(64 * codes.shape[0] * width),
    )(codes)


def blank_body(out):
    out[...] = jnp.zeros_like(out)


def blank(rows):
    early = pl.CostEstimate(flops=1 << 34, bytes_accessed=1 << 25, transcendentals=0)
    return call(blank_body, in_vmem((rows, LANES)), [], cost_estimate=early)()


def stack_body(*refs):
    *blocks, out = refs
    out[...] = jnp.concatenate([block[...] for block in blocks], axis=0)


def stack(blocks):
    rows = sum(block.shape[0] for block in blocks)
    return call(stack_body, in_vmem((rows, LANES)), [WHOLE] * len(blocks))(*blocks)


def lookup(table, index, out):
    height = table.shape[0]
    rhs, count = index.shape
    half = LANES // 2
    exact = jnp.bfloat16 if 2 * height <= 256 else jnp.float32
    row = lax.broadcasted_iota(jnp.int32, (2 * height, count), 0).astype(exact)
    lane = lax.broadcasted_iota(jnp.int32, (half, count), 0)
    halves = table.T
    left = bf16_pieces(jnp.concatenate([halves[:half], halves[half:]], axis=1))
    one, none = jnp.ones((), exact), jnp.zeros((), exact)
    for b in range(rhs):
        places = index[b : b + 1, :]
        wanted = places // LANES + height * (places // half % 2)
        chosen = jnp.where(row == wanted.astype(jnp.float32).astype(exact), one, none)
        values = add_pieces(
            jnp.dot(left, chosen.astype(jnp.bfloat16), preferred_element_type=jnp.float32)
        )
        out[b : b + 1, :] = jnp.sum(
            jnp.where(lane == places % half, values, 0.0), axis=0, keepdims=True
        )


def slab_body(perm, direction, resid, codes, pct, *refs, axis):
    *table, shuffled, sums = refs
    rhs = direction.shape[0]
    table = jnp.concatenate([block[...] for block in by_distance(table, GATHER_ORDER)], axis=0)
    shard = table.size // lax.axis_size(axis)
    lookup(table, perm[...] ^ (lax.axis_index(axis) * shard), shuffled)
    mean, scale = spread(pct[...])
    straight = direction[...]
    both = jnp.concatenate([straight, shuffled[...] * straight], axis=0)
    product = add_pieces(
        jnp.dot(bf16_pieces(both), codes[...], preferred_element_type=jnp.float32)
    )
    fold(scale * (product - mean * jnp.sum(both, axis=1, keepdims=True)), sums)
    left = resid[...]
    norm = jnp.sum(left * left, axis=1, keepdims=True)
    length = jnp.sum(straight * straight, axis=1, keepdims=True)
    lane = lax.broadcasted_iota(jnp.int32, (rhs, LANES), 1)
    sums[-rhs:, :] = jnp.where(lane < LANES // 2, norm, length)


def slab_sums(table, perm, direction, resid, codes, pct, axis):
    rhs, slab = direction.shape[0], codes.shape[1]
    return call(
        functools.partial(slab_body, axis=axis),
        [in_vmem(perm.shape), in_vmem((2 * rhs * slab // LANES + rhs, LANES))],
        [WHOLE] * (5 + len(table)),
    )(perm, direction, resid, codes, pct, *table)


def kernel_body(sums, flipped, pct, shuffled, var_comp, out, norms, *, slab_total):
    rhs, count = shuffled.shape
    weights = unfold(sums[:-rhs, :], 2 * rhs)
    squares = jnp.sum(weights * weights, axis=1, keepdims=True)
    mean, scale = spread(pct[...])
    weights = scale * weights
    product = add_pieces(
        jnp.dot(bf16_pieces(weights), flipped[...], preferred_element_type=jnp.float32)
    ) - jnp.sum(mean * weights, axis=1, keepdims=True)
    share = 1.0 / slab_total
    out[:, :count] = (
        var_comp[1] * product[:rhs] + var_comp[2] * shuffled[...] * product[rhs:]
    ) * share
    energy = (var_comp[1] * squares[:rhs] + var_comp[2] * squares[rhs:]) * share
    out[:, count:] = jnp.broadcast_to(energy, (rhs, LANES))
    half = LANES // 2
    norms[:rhs, :] = jnp.broadcast_to(sums[-rhs:, :][:, :1], (rhs, LANES))
    norms[rhs:, :] = jnp.broadcast_to(sums[-rhs:, :][:, half : half + 1], (rhs, LANES))


def kernel_part(sums, flipped, pct, shuffled, var_comp, slab_total):
    rhs, count = shuffled.shape
    return call(
        functools.partial(kernel_body, slab_total=slab_total),
        [in_vmem((rhs, count + LANES)), in_vmem((2 * rhs, LANES))],
        [WHOLE] * 4 + [SCALARS],
    )(sums, flipped, pct, shuffled, var_comp)


def step_body(applied, norms, shuffled, direction, resid, solution, codes, pct, empty, var_comp,
              new_solution, new_resid, scores, *, root):
    rhs, count = shuffled.shape
    straight = direction[...]
    image = var_comp[0] * straight + applied[:, :count]
    curvature = var_comp[0] * norms[rhs:, :1] + applied[:, count : count + 1]
    alpha = norms[:rhs, :1] / curvature
    left = resid[...] - alpha * image
    new_resid[...] = left
    new_solution[...] = solution[...] + alpha * straight
    both = jnp.concatenate([left, shuffled[...] * left], axis=0)
    mean, scale = spread(pct[...])
    product = add_pieces(
        jnp.dot(bf16_pieces(both), codes[...], preferred_element_type=jnp.float32)
    )
    product -= mean * jnp.sum(both, axis=1, keepdims=True)
    fold((scale / root) * product, scores)
    scores[-rhs:, :] = empty[...] + jnp.sum(left * left, axis=1, keepdims=True)


def step(applied, norms, shuffled, direction, resid, solution, codes, pct, empty, var_comp, root):
    rhs, count = shuffled.shape
    return call(
        functools.partial(step_body, root=root),
        [
            in_vmem((rhs, count)),
            in_vmem((rhs, count)),
            in_vmem((2 * rhs * codes.shape[1] // LANES + rhs, LANES)),
        ],
        [WHOLE] * 9 + [SCALARS],
    )(applied, norms, shuffled, direction, resid, solution, codes, pct, empty, var_comp)


def finish_body(norms, new_resid, direction, *refs):
    *parts, new_direction, scores = refs
    rhs = direction.shape[0]
    total = add_parts([part[...] for part in by_distance(parts, SCORE_ORDER)])
    scores[...] = unfold(total[:-rhs], 2 * rhs)
    ratio = total[-rhs:, :1] / norms[:rhs, :1]
    new_direction[...] = new_resid[...] + ratio * direction[...]


def finish(parts, norms, new_resid, direction):
    rhs = direction.shape[0]
    tests = (parts[0].shape[0] - rhs) // (2 * rhs) * LANES
    return call(
        finish_body,
        [
            jax.ShapeDtypeStruct(direction.shape, jnp.float32),
            jax.ShapeDtypeStruct((2 * rhs, tests), jnp.float32),
        ],
        [WHOLE] * (3 + len(parts)),
    )(norms, new_resid, direction, *parts)


def add_body(*refs):
    *parts, out = refs
    out[...] = add_parts([part[...] for part in by_distance(parts, SLAB_ORDER)])


def add_up(parts):
    return call(add_body, in_vmem(parts[0].shape), [WHOLE] * len(parts))(*parts)


def swap(x, axis, distance):
    size = lax.axis_size(axis)
    return lax.ppermute(x, axis, [(i, i ^ distance) for i in range(size)])


def swaps(x, axis, width, unit, order):
    return [swap(x, axis, k * unit) for k in order if k < width]


def by_distance(parts, order):
    order = [k for k in order if k < len(parts)]
    return [parts[0]] + [parts[1 + order.index(k)] for k in range(1, len(parts))]


def add_parts(parts):
    if len(parts) == 4:
        return (parts[0] + parts[1]) + (parts[2] + parts[3])
    return sum(parts[1:], parts[0])


def sum_parts(x, axis, widths, order, unit=1):
    parts = [x]
    for width in widths(lax.axis_size(axis) // unit):
        held = add_parts(by_distance(parts, order))
        parts = [held] + swaps(held, axis, width, unit, order)
        unit *= width
    return parts


def sum_all(x, axis, widths):
    return add_parts(by_distance(sum_parts(x, axis, widths, (1,)), (1,)))


def gather_all(x, axis, widths, beside):
    blocks = [x]
    unit = 1
    for width in widths(lax.axis_size(axis)):
        held = blocks[0] if len(blocks) == 1 else stack(by_distance(blocks, GATHER_ORDER))
        blocks = [held] + swaps(held, axis, width, unit, GATHER_ORDER)
        if unit == 1:
            beside, blocks[1] = lax.optimization_barrier((beside, blocks[1]))
        unit *= width
    return blocks, beside


def pairs_then_fours(size):
    bits = size.bit_length() - 1
    return [2] * (bits % 2) + [4] * (bits // 2)


def pairs(size):
    return [2] * (size.bit_length() - 1)


def local(
    geno, allele_pct, test_geno, test_pct, exposure, perm, var_comp, solution, resid, direction
):
    rhs, count = resid.shape
    slab = geno.shape[1]
    tests = test_geno.shape[1]
    slab_total = float(slab * lax.axis_size("var"))
    root = math.sqrt(count * lax.axis_size("samp"))
    pct = allele_pct.reshape(1, slab)
    table, empty = gather_all(
        exposure.reshape(-1, LANES), "samp", pairs_then_fours, blank(rhs)
    )
    codes = cast_codes(geno)
    shuffled, sums = slab_sums(table, perm, direction, resid, codes, pct, "samp")
    sums = sums + swap(sums, "samp", 1)
    codes, sums = lax.optimization_barrier((codes, sums))
    flipped = flip_codes(codes, 0, slab)
    parts = sum_parts(sums, "samp", pairs_then_fours, SLAB_ORDER, 2)
    sums = add_up(parts)
    applied, norms = kernel_part(sums, flipped, pct, shuffled, var_comp, slab_total)
    applied = sum_all(applied, "var", pairs)
    test_codes = cast_codes(test_geno)
    new_solution, new_resid, scores = step(
        applied, norms, shuffled, direction, resid, solution, test_codes,
        test_pct.reshape(1, tests), empty, var_comp, root,
    )
    parts = sum_parts(scores, "samp", pairs_then_fours, SCORE_ORDER)
    new_direction, scores = finish(parts, norms, new_resid, direction)
    return (new_solution, new_resid, new_direction, scores)


def solution(mesh):
    return jax.shard_map(
        local,
        mesh=mesh,
        in_specs=(
            P("samp", "var"),
            P("var"),
            P("samp", "var"),
            P("var"),
            P("samp"),
            P(None, "samp"),
            P(),
            P(None, "samp"),
            P(None, "samp"),
            P(None, "samp"),
        ),
        out_specs=(P(None, "samp"), P(None, "samp"), P(None, "samp"), P(None, "var")),
        check_vma=False,
    )
```
